512 devices in a mesh: row: 16 (over x, z_hi), col: 32 (over y, z_lo, core).
Axes of the slice: x: 4, y: 4, z: 16 (z_hi: 4, z_lo: 4; z = z_hi * 4 + z_lo), core: 2. Of those that a mesh axis runs over, the one named last changes fastest.
Arguments:
- nodes: bfloat16 [16384, 256], P(('row', 'col')), may hold values from -6 to 6
- harmonics: bfloat16 [16, 512, 25, 128], P('row', 'col'), may hold values from -6 to 6
- grad_blocks: bfloat16 [16, 512, 169, 128], P('row', 'col'), may hold values from -6 to 6
- pair_rows: int32 [16, 512, 128], P('row', 'col'), may hold values from 0 to 1023
- pair_cols: int32 [16, 512, 128], P('row', 'col'), may hold values from 0 to 511, as said below
- pair_mask: int32 [16, 512, 128], P('row', 'col'), may hold values 0 or 1
- block_counts: int32 [16, 32], P('row', 'col'), may hold values from 1 to 16
- w_left: bfloat16 [256, 256], replicated, may hold values from -0.375 to 0.375
- w_right: bfloat16 [256, 256], replicated, may hold values from -0.375 to 0.375
- w_harm: bfloat16 [25, 256], replicated, may hold values from -1.25 to 1.25
- w_out: bfloat16 [169, 256], replicated, may hold values from -0.375 to 0.375
Outputs:
- grad_nodes: float32 [16384, 256], P(('row', 'col'))
- grad_w_left: float32 [256, 256], replicated
- grad_w_right: float32 [256, 256], replicated
- grad_w_harm: float32 [25, 256], replicated
- grad_w_out: float32 [169, 256], replicated
The draws below stay inside these ranges and needn't reach their ends.
Inputs may be any that keep to these rules, and one draw needn't show every extreme that they name: pair_cols // 32 differs by at most one from the row index r of the pair's grid cell.
All inputs are finite; a program needn't handle non-finite values. No bound on the sum of `pair_mask` on one device may be relied on, other than what follows from the above.
Results may differ from the reference program's by a relative error of at most 0.0032.
Values may be sent and summed in bfloat16 or wider, within the bound.
No kernel may reach another device: no remote copies, remote signals or barrier semaphores. Data moves between devices by JAX's collectives and lax.ppermute only.
A program may use at most 64 MiB of HBM per device.

```python
import jax
import jax.numpy as jnp
from jax import lax

C = 256
ORB2 = 169
NHARM = 25
PAIR = 128
ATOMS_DEV = 32
MAXB = 16
ROWGROUPS = 16
COLGROUPS = 32
ATOMS = 16384
ROW_ATOMS = 1024
BLOCKS = 512


def draw_pair_cols(key, part):
    key = jax.random.fold_in(key, 11)
    shape = (ROWGROUPS, BLOCKS, PAIR)
    off_key, pos_key = jax.random.split(key)
    offset = jax.random.randint(off_key, shape, -1, 2, dtype=jnp.int32)
    row_of = lax.broadcasted_iota(jnp.int32, shape, 0)
    shard = jnp.clip(row_of + offset, 0, ROWGROUPS - 1)
    position = jax.random.randint(pos_key, shape, 0, ATOMS_DEV, dtype=jnp.int32)
    return shard * ATOMS_DEV + position


def draw_block_counts(key, part):
    key = jax.random.fold_in(key, 23)
    base_key, pick_key = jax.random.split(key)
    base = jax.random.randint(base_key, (ROWGROUPS * COLGROUPS,), 0, MAXB, dtype=jnp.int32)
    counts = 1 + base * base // MAXB
    chosen = jax.random.randint(pick_key, (), 0, ROWGROUPS * COLGROUPS, dtype=jnp.int32)
    counts = counts.at[chosen].set(MAXB)
    return counts.reshape(ROWGROUPS, COLGROUPS)


def with_ends(entries, stream_key, least, high):
    dims = entries.shape
    index_at = [jax.random.randint(jax.random.fold_in(stream_key, axis), (), 0, dims[axis]) for axis in range(len(dims))]
    entries = entries.at[tuple(index_at)].set(least)
    longest = dims.index(max(dims))
    index_at[longest] = (index_at[longest] + 1) % dims[longest]
    return entries.at[tuple(index_at)].set(high)


def steps_of(rng, extent, cuts, low, high):
    gain = 1.0
    for axis_at, shards_of in cuts:
        steps = jax.random.uniform(jax.random.fold_in(jax.random.fold_in(rng, 6), axis_at), (shards_of,), jnp.float32, low / len(cuts), high / len(cuts))
        gain = gain * jnp.repeat(jnp.exp(steps), extent[axis_at] // shards_of).reshape((-1,) + (1,) * (len(extent) - 1 - axis_at))
    return gain


def scatter_about(rng, extent, deviation, limit, pieces=(), held_as=jnp.bfloat16):
    drawn = jax.random.normal(rng, extent, jnp.float32) * deviation
    if len(pieces) > 0:
        drawn = steps_of(rng, extent, pieces, -0.22, 0.18) * drawn
    return jnp.clip(drawn, min=-limit, max=limit).astype(held_as)


def setup_inputs(seed: int = 0) -> dict:
    splits = jax.random.split(jax.random.key(seed), 12)
    nodes = scatter_about(splits[0], (ATOMS, C), 1.0, 6.0, ((0, 512),))
    harmonics = scatter_about(splits[1], (ROWGROUPS, BLOCKS, NHARM, PAIR), 1.0, 6.0, ((0, 16), (1, 32)))
    grad_blocks = scatter_about(splits[2], (ROWGROUPS, BLOCKS, ORB2, PAIR), 1.0, 6.0, ((0, 16), (1, 32)))
    pair_rows = with_ends(jax.random.randint(splits[3], (ROWGROUPS, BLOCKS, PAIR), 0, ROW_ATOMS), jax.random.fold_in(splits[3], 1), 0, ROW_ATOMS - 1).astype(jnp.int32)
    pair_cols = draw_pair_cols(jax.random.fold_in(splits[11], 71), 0)
    pair_mask = with_ends((jax.random.randint(splits[5], (ROWGROUPS, BLOCKS, PAIR), 0, 8) < 7).astype(jnp.int32), jax.random.fold_in(splits[5], 1), 0, 1)
    block_counts = draw_block_counts(jax.random.fold_in(splits[11], 71), 0)
    w_left = scatter_about(splits[7], (C, C), C ** -0.5, 0.375)
    w_right = scatter_about(splits[8], (C, C), C ** -0.5, 0.375)
    w_harm = scatter_about(splits[9], (NHARM, C), NHARM ** -0.5, 1.25)
    w_out = scatter_about(splits[10], (ORB2, C), C ** -0.5, 0.375)
    return dict(nodes=nodes, harmonics=harmonics, grad_blocks=grad_blocks, pair_rows=pair_rows, pair_cols=pair_cols, pair_mask=pair_mask, block_counts=block_counts, w_left=w_left, w_right=w_right, w_harm=w_harm, w_out=w_out)


def reference(nodes, harmonics, grad_blocks, pair_rows, pair_cols, pair_mask, block_counts, w_left, w_right, w_harm, w_out):
    row_atoms = ATOMS_DEV * COLGROUPS
    width = nodes.shape[1]
    u_atoms = jnp.dot(nodes, w_left, preferred_element_type=jnp.float32)
    v_atoms = jnp.dot(nodes, w_right, preferred_element_type=jnp.float32)
    harm_weight = w_harm.astype(jnp.float32)
    out_weight = w_out.astype(jnp.float32)

    def cell(carry, cell_id):
        sum_u, sum_v, grad_out, grad_harm = carry
        rgrp = cell_id // COLGROUPS
        cgrp = cell_id % COLGROUPS
        start = (cgrp * MAXB).astype(jnp.int32)

        def pick(table):
            line = lax.dynamic_index_in_dim(table, rgrp, 0, keepdims=False)
            return lax.dynamic_slice_in_dim(line, start, MAXB, 0)

        rows = pick(pair_rows)
        cols = pick(pair_cols)
        masks = pick(pair_mask)
        harm = pick(harmonics)
        grads = pick(grad_blocks)
        count_line = lax.dynamic_index_in_dim(block_counts, rgrp, 0, keepdims=False)
        count = lax.dynamic_index_in_dim(count_line, cgrp, 0, keepdims=False)
        live = jnp.arange(MAXB, dtype=jnp.int32) < count
        weight_mask = (masks * live[:, None].astype(jnp.int32)).astype(jnp.bfloat16)
        g_masked = grads * weight_mask[:, None, :]
        a_glob = (rgrp * row_atoms + rows).reshape(-1).astype(jnp.int32)
        b_glob = ((cols // ATOMS_DEV) * row_atoms + cgrp * ATOMS_DEV + cols % ATOMS_DEV).reshape(-1).astype(jnp.int32)
        u_pair = u_atoms[a_glob]
        v_pair = v_atoms[b_glob]
        embed = jnp.einsum("bmp,mk->bpk", harm.astype(jnp.float32), harm_weight).reshape(-1, width)
        g_float = g_masked.astype(jnp.float32)
        grad_z = jnp.einsum("bop,ok->bpk", g_float, out_weight).reshape(-1, width)
        z_pair = (u_pair * v_pair * embed).astype(jnp.bfloat16).reshape(MAXB, -1, width)
        grad_out = grad_out + jnp.einsum("bop,bpk->ok", g_float, z_pair.astype(jnp.float32))
        grad_e = (grad_z * u_pair * v_pair).astype(jnp.bfloat16).reshape(MAXB, -1, width)
        grad_harm = grad_harm + jnp.einsum("bmp,bpk->mk", harm.astype(jnp.float32), grad_e.astype(jnp.float32))
        sum_u = sum_u.at[a_glob].add(grad_z * v_pair * embed)
        sum_v = sum_v.at[b_glob].add(grad_z * u_pair * embed)
        return (sum_u, sum_v, grad_out, grad_harm), None

    start_carry = (jnp.zeros(u_atoms.shape, jnp.float32), jnp.zeros(u_atoms.shape, jnp.float32),
                   jnp.zeros(w_out.shape, jnp.float32), jnp.zeros(w_harm.shape, jnp.float32))
    cells = jnp.arange(ROWGROUPS * COLGROUPS, dtype=jnp.int32)
    (sum_u, sum_v, grad_out, grad_harm), _ = lax.scan(cell, start_carry, cells)
    highest = lax.Precision.HIGHEST
    left_float = w_left.astype(jnp.float32)
    right_float = w_right.astype(jnp.float32)
    node_float = nodes.astype(jnp.float32)
    grad_nodes = jnp.dot(sum_u, left_float.T, precision=highest) + jnp.dot(sum_v, right_float.T, precision=highest)
    grad_left = jnp.dot(node_float.T, sum_u, precision=highest)
    grad_right = jnp.dot(node_float.T, sum_v, precision=highest)
    return (grad_nodes, grad_left, grad_right, grad_harm, grad_out)
```

```python
import jax
import jax.numpy as jnp
from jax import lax
from jax.experimental import pallas as pl
from jax.experimental.pallas import tpu as pltpu
from jax.sharding import PartitionSpec as P

F32, BF16 = jnp.float32, jnp.bfloat16
VMEM = pl.BlockSpec(memory_space=pltpu.VMEM)
SMEM = pl.BlockSpec(memory_space=pltpu.SMEM)
PARAMS = pltpu.CompilerParams(vmem_limit_bytes=48 * 1024 * 1024)
BOTH = ("row", "col")


def like(*shape):
    return jax.ShapeDtypeStruct(shape, F32)


def dot(a, b, da, db):
    return lax.dot_general(a, b, (((da,), (db,)), ((), ())), preferred_element_type=F32)


def halves(x):
    high = x.astype(BF16)
    return high, (x - high.astype(F32)).astype(BF16)


def pair_kernel(
    places, rows, cols, mask, harm, grads, own, other, column_nodes, w_left, w_right, w_harm, w_out,
    keep, send, sum_v, u_parts, v_parts, sum_u, weights,
):
    count, column_base, core = places[0], places[1], places[2]
    width = w_left.shape[0]
    half = own.shape[0]
    shard = column_nodes.shape[0] // 3
    pairs = 2 * mask.shape[1]
    orbitals, harmonics = w_out.shape[0], w_harm.shape[0]
    for first, nodes in ((0, own), (half, other)):
        high, low = halves(dot(w_left[...], nodes[...], 0, 1))
        u_parts[:width, first : first + half] = high
        u_parts[width:, first : first + half] = low
    high, low = halves(dot(w_right[...], column_nodes[...], 0, 1))
    v_parts[:width] = high
    v_parts[width:] = low
    for total in (sum_u, sum_v, weights):
        total[...] = jnp.zeros_like(total)
    at_out = 2 * width
    at_harm = at_out + 176

    def line(ref, first):
        return jnp.concatenate([ref[pl.ds(first, 1), :], ref[pl.ds(first + 1, 1), :]], axis=1)

    def step(i, carry):
        first = 2 * i
        second = (first + 1 < count).astype(jnp.int32)
        live = jnp.concatenate(
            [mask[pl.ds(first, 1), :], mask[pl.ds(first + 1, 1), :] * second], axis=1
        )
        g = jnp.concatenate([grads[first], grads[first + 1]], axis=1)
        g = g * live.astype(F32).astype(BF16)
        h = jnp.concatenate([harm[first], harm[first + 1]], axis=1)
        atom = line(rows, first)
        owner = lax.shift_right_logical(atom, 5)
        away = jnp.bitwise_and(owner, 1) != core
        place = lax.shift_right_logical(owner, 1) * shard + jnp.bitwise_and(atom, shard - 1)
        place = place + jnp.where(away, half, 0)
        at_u = lax.broadcasted_iota(jnp.int32, (2 * half, pairs), 0) == place
        at_v = lax.broadcasted_iota(jnp.int32, (3 * shard, pairs), 0) == (
            line(cols, first) - column_base
        )
        pick_u = at_u.astype(F32).astype(BF16)
        pick_v = at_v.astype(F32).astype(BF16)
        parts = dot(u_parts[...], pick_u, 1, 0)
        u = parts[:width] + parts[width:]
        parts = dot(v_parts[...], pick_v, 1, 0)
        v = parts[:width] + parts[width:]
        e = dot(w_harm[...], h, 0, 0)
        gz = dot(w_out[...], g, 0, 0)
        uv = u * v
        weights[at_out : at_out + orbitals] += dot(g, (uv * e).astype(BF16), 1, 1)
        weights[at_harm : at_harm + harmonics] += dot(h, (gz * uv).astype(BF16), 1, 1)
        ge = gz * e
        high, low = halves(ge * v)
        sum_u[...] += dot(pick_u, high, 1, 1) + dot(pick_u, low, 1, 1)
        high, low = halves(ge * u)
        sum_v[...] += dot(pick_v, high, 1, 1) + dot(pick_v, low, 1, 1)
        return carry

    lax.fori_loop(0, lax.shift_right_logical(count + 1, 1), step, 0)
    left = jnp.zeros((width, width), F32)
    for first, nodes in ((0, own), (half, other)):
        for part in halves(sum_u[first : first + half]):
            left = left + dot(nodes[...], part, 0, 0)
    weights[:width] = left
    right = jnp.zeros((width, width), F32)
    for part in halves(sum_v[...]):
        right = right + dot(column_nodes[...], part, 0, 0)
    weights[width : 2 * width] = right
    chips, chunk = keep.shape[0], keep.shape[1]
    share = chunk - shard
    for chip in range(chips):
        keep[chip, :shard] = sum_u[chip * shard : (chip + 1) * shard]
        send[chip, :shard] = sum_u[half + chip * shard : half + (chip + 1) * shard]
        for to, which in ((keep, core), (send, 1 - core)):
            start = pl.multiple_of((which * chips + chip) * share, 8)
            to[chip, shard:] = weights[pl.ds(start, share), :]


def pair_sums(places, rows, cols, mask, harm, grads, own, other, column_nodes, weights_in, chips, share):
    width = own.shape[1]
    shard = column_nodes.shape[0] // 3
    half = own.shape[0]
    return pl.pallas_call(
        pair_kernel,
        out_shape=(
            like(chips, shard + share, width),
            like(chips, shard + share, width),
            like(3 * shard, width),
        ),
        in_specs=[SMEM] + [VMEM] * 12,
        out_specs=(VMEM,) * 3,
        scratch_shapes=[
            pltpu.VMEM((2 * width, 2 * half), BF16),
            pltpu.VMEM((2 * width, 3 * shard), BF16),
            pltpu.VMEM((2 * half, width), F32),
            pltpu.VMEM((2 * chips * share, width), F32),
        ],
        compiler_params=PARAMS,
    )(places, rows, cols, mask, harm, grads, own, other, column_nodes, *weights_in)


def node_kernel(parts, middle, upper, lower, w_left, w_right, grad_nodes, shares):
    shard = middle.shape[0]
    total = parts[0].astype(F32)
    for chip in range(1, parts.shape[0]):
        total = total + parts[chip].astype(F32)
    out = jnp.zeros(grad_nodes.shape, F32)
    columns = middle[...] + upper[...] + lower[...]
    for sums, weight in ((total[:shard], w_left), (columns, w_right)):
        for part in halves(sums):
            out = out + dot(part, weight[...], 1, 1)
    grad_nodes[...] = out
    for x in range(shares.shape[0]):
        shares[x] = total[shard:]


def node_grads(parts, middle, upper, lower, w_left, w_right, copies):
    shard, width = middle.shape
    return pl.pallas_call(
        node_kernel,
        out_shape=(like(shard, width), like(copies, parts.shape[1] - shard, width)),
        in_specs=[VMEM] * 6,
        out_specs=(VMEM,) * 2,
        compiler_params=PARAMS,
    )(parts, middle, upper, lower, w_left, w_right)


def sum_kernel(parts, out):
    total = parts[0]
    for i in range(1, parts.shape[0]):
        total = total + parts[i]
    for i in range(out.shape[0]):
        out[i] = total.astype(out.dtype)


def summed(parts, copies, dtype):
    return pl.pallas_call(
        sum_kernel,
        out_shape=jax.ShapeDtypeStruct((copies,) + parts.shape[1:], dtype),
        in_specs=[VMEM],
        out_specs=VMEM,
        compiler_params=PARAMS,
    )(parts)


def split_kernel(core, own, other, left, right, harm, out, whole):
    chips, share = own.shape[0], own.shape[1]
    width = left.shape[0]
    for which, part in ((core[0], own), (1 - core[0], other)):
        for chip in range(chips):
            start = pl.multiple_of((which * chips + chip) * share, 8)
            whole[pl.ds(start, share), :] = part[chip].astype(F32)
    left[...] = whole[:width]
    right[...] = whole[width : 2 * width]
    at_out = 2 * width
    out[...] = whole[at_out : at_out + out.shape[0]]
    at_harm = at_out + 176
    harm[...] = whole[at_harm : at_harm + harm.shape[0]]


def split(core, own, other, harmonics, orbitals):
    chips, share, width = own.shape
    return pl.pallas_call(
        split_kernel,
        out_shape=(
            like(width, width), like(width, width), like(harmonics, width), like(orbitals, width),
        ),
        in_specs=[SMEM, VMEM, VMEM],
        out_specs=(VMEM,) * 4,
        scratch_shapes=[pltpu.VMEM((2 * chips * share, width), F32)],
        compiler_params=PARAMS,
    )(core, own, other)


def groups(size, bits):
    mask = sum(bits)
    found = {}
    for i in range(size):
        found.setdefault(i & ~mask, []).append(i)
    return list(found.values())


def exchange(blocks, axis, bits):
    return lax.all_to_all(
        blocks, axis, 0, 0, tiled=True, axis_index_groups=groups(lax.axis_size(axis), bits)
    )


def swapped(block):
    return lax.ppermute(block, "col", [(i, i ^ 1) for i in range(lax.axis_size("col"))])


def shifted(block, distance):
    devices = range(lax.axis_size("row"))
    return lax.ppermute(
        block, "row", [(i, i + distance) for i in devices if i + distance in devices]
    )


def repeated(block, copies):
    return jnp.broadcast_to(block[None], (copies,) + block.shape)


def body(
    nodes,
    harmonics,
    grad_blocks,
    pair_rows,
    pair_cols,
    pair_mask,
    block_counts,
    w_left,
    w_right,
    w_harm,
    w_out,
):
    shard, width = nodes.shape
    chips = lax.axis_size("col") // 2
    share = 24
    core = jnp.bitwise_and(lax.axis_index("col"), 1)
    before = shifted(nodes, 1)
    after = shifted(nodes, -1)
    own = exchange(repeated(nodes, chips), "col", (2, 4, 8, 16)).reshape(-1, width)
    other = swapped(own)
    column_nodes = jnp.concatenate([before, nodes, after])
    places = jnp.stack(
        [block_counts[0, 0], (lax.axis_index("row") - 1) * shard, core]
    ).astype(jnp.int32)
    keep, send, sum_v = pair_sums(
        places, pair_rows[0], pair_cols[0], pair_mask[0], harmonics[0], grad_blocks[0],
        own, other, column_nodes, (w_left, w_right, w_harm, w_out), chips, share,
    )
    upper = shifted(sum_v[:shard], -1)
    lower = shifted(sum_v[2 * shard :], 1)
    parts = (keep + swapped(send)).astype(BF16)
    parts = exchange(parts, "col", (2, 4, 8, 16))
    grad_nodes, shares = node_grads(
        parts, sum_v[shard : 2 * shard], upper, lower, w_left, w_right, 4
    )
    shares = summed(exchange(shares, "row", (4, 8)), 4, F32)
    shares = summed(exchange(shares, "row", (1, 2)), chips, BF16)
    own_shares = exchange(shares, "col", (2, 4, 8, 16))
    left, right, harm, out = split(
        core.reshape(1), own_shares, swapped(own_shares), w_harm.shape[0], w_out.shape[0]
    )
    return (grad_nodes, left, right, harm, out)


def solution(mesh):
    return jax.shard_map(
        body,
        mesh=mesh,
        in_specs=(
            P(BOTH, None),
            P("row", "col", None, None),
            P("row", "col", None, None),
            P("row", "col", None),
            P("row", "col", None),
            P("row", "col", None),
            P("row", "col"),
            P(),
            P(),
            P(),
            P(),
        ),
        out_specs=(P(BOTH, None), P(), P(), P(), P()),
        check_vma=False,
    )
```

```python
import jax
import jax.numpy as jnp
from jax import lax
from jax.experimental import pallas as pl
from jax.experimental.pallas import tpu as pltpu
from jax.sharding import PartitionSpec as P

F32, BF16 = jnp.float32, jnp.bfloat16
VMEM = pl.BlockSpec(memory_space=pltpu.VMEM)
SMEM = pl.BlockSpec(memory_space=pltpu.SMEM)
PARAMS = pltpu.CompilerParams(vmem_limit_bytes=48 * 1024 * 1024)
BOTH = ("row", "col")
BLOCKS_PER_STEP = 8
OUT_ROWS = 176
X_BITS, Z_BITS, CHIP_BITS, COL_BITS = (4, 8), (1, 2), (2, 4, 8, 16), (1, 2, 4, 8, 16)


def like(*shape):
    return jax.ShapeDtypeStruct(shape, F32)


def dot(a, b, da, db):
    return lax.dot_general(a, b, (((da,), (db,)), ((), ())), preferred_element_type=F32)


def halves(x):
    high = x.astype(BF16)
    return high, (x - high.astype(F32)).astype(BF16)


def pair_kernel(
    places, rows, cols, mask, harm, grads, row_nodes, column_nodes, w_left, w_right, w_harm, w_out,
    keep, send, sum_v, u_parts, v_parts, harm_t, out_t, sum_u, weights,
):
    count, column_base, core = places[0], places[1], places[2]
    width = w_left.shape[0]
    atoms, near = row_nodes.shape[0], column_nodes.shape[0]
    shard = near // 3
    pairs = BLOCKS_PER_STEP * mask.shape[1]
    orbitals, harmonics = w_out.shape[0], w_harm.shape[0]
    for parts, weight, nodes in ((u_parts, w_left, row_nodes), (v_parts, w_right, column_nodes)):
        high, low = halves(dot(weight[...], nodes[...], 0, 1))
        parts[:width] = high
        parts[width:] = low
    harm_t[...] = w_harm[...].astype(F32).T.astype(BF16)
    out_t[...] = w_out[...].astype(F32).T.astype(BF16)
    for total in (sum_u, sum_v, weights):
        total[...] = jnp.zeros_like(total)
    at_out = 2 * width
    at_harm = at_out + OUT_ROWS

    def line(ref, first):
        return jnp.concatenate(
            [ref[pl.ds(first + k, 1), :] for k in range(BLOCKS_PER_STEP)], axis=1
        )

    def step(i, carry):
        first = BLOCKS_PER_STEP * i
        live = jnp.concatenate(
            [
                mask[pl.ds(first + k, 1), :] * (first + k < count).astype(jnp.int32)
                for k in range(BLOCKS_PER_STEP)
            ],
            axis=1,
        )
        g = jnp.concatenate([grads[first + k] for k in range(BLOCKS_PER_STEP)], axis=1)
        g = g * live.astype(F32).astype(BF16)
        h = jnp.concatenate([harm[first + k] for k in range(BLOCKS_PER_STEP)], axis=1)
        at_u = lax.broadcasted_iota(jnp.int32, (atoms, pairs), 0) == line(rows, first)
        at_v = lax.broadcasted_iota(jnp.int32, (near, pairs), 0) == line(cols, first) - column_base
        pick_u = at_u.astype(F32).astype(BF16)
        pick_v = at_v.astype(F32).astype(BF16)
        parts = dot(u_parts[...], pick_u, 1, 0)
        u = parts[:width] + parts[width:]
        parts = dot(v_parts[...], pick_v, 1, 0)
        v = parts[:width] + parts[width:]
        e = dot(harm_t[...], h, 1, 0)
        gz = dot(out_t[...], g, 1, 0)
        uv = u * v
        weights[at_out : at_out + orbitals] += dot(g, (uv * e).astype(BF16), 1, 1)
        weights[at_harm : at_harm + harmonics] += dot(h, (gz * uv).astype(BF16), 1, 1)
        ge = gz * e
        high, low = halves(ge * v)
        sum_u[...] += dot(pick_u, high, 1, 1) + dot(pick_u, low, 1, 1)
        high, low = halves(ge * u)
        sum_v[...] += dot(pick_v, high, 1, 1) + dot(pick_v, low, 1, 1)
        return carry

    lax.fori_loop(0, lax.div(count + BLOCKS_PER_STEP - 1, BLOCKS_PER_STEP), step, 0)
    for at, nodes, sums in ((0, row_nodes, sum_u), (width, column_nodes, sum_v)):
        high, low = halves(sums[...])
        weights[at : at + width] = dot(nodes[...], high, 0, 0) + dot(nodes[...], low, 0, 0)
    chips, chunk = keep.shape[0], keep.shape[1]
    share = chunk - shard
    for chip in range(chips):
        for to, which in ((keep, core), (send, 1 - core)):
            start = pl.multiple_of((2 * chip + which) * shard, 8)
            to[chip, :shard] = sum_u[pl.ds(start, shard), :]
            start = pl.multiple_of((which * chips + chip) * share, 8)
            to[chip, shard:] = weights[pl.ds(start, share), :]


def pair_sums(places, rows, cols, mask, harm, grads, row_nodes, column_nodes, weights_in, chips, share):
    atoms, width = row_nodes.shape
    near = column_nodes.shape[0]
    chunk = near // 3 + share
    w_harm, w_out = weights_in[2:]
    return pl.pallas_call(
        pair_kernel,
        out_shape=(like(chips, chunk, width), like(chips, chunk, width), like(near, width)),
        in_specs=[SMEM] + [VMEM] * 11,
        out_specs=(VMEM,) * 3,
        scratch_shapes=[
            pltpu.VMEM((2 * width, atoms), BF16),
            pltpu.VMEM((2 * width, near), BF16),
            pltpu.VMEM(w_harm.shape[::-1], BF16),
            pltpu.VMEM(w_out.shape[::-1], BF16),
            pltpu.VMEM((atoms, width), F32),
            pltpu.VMEM((2 * chips * share, width), F32),
        ],
        compiler_params=PARAMS,
    )(places, rows, cols, mask, harm, grads, row_nodes, column_nodes, *weights_in)


def total_of(parts):
    total = parts[0].astype(F32)
    for i in range(1, parts.shape[0]):
        total = total + parts[i].astype(F32)
    return total


def weighted(sums, weight):
    high, low = halves(sums)
    return dot(high, weight[...], 1, 1) + dot(low, weight[...], 1, 1)


def when(condition, block):
    return jnp.where(condition, block, jnp.zeros_like(block))


def across_x_kernel(places, parts, sum_v, w_left, row_part, out):
    x, z = places[0], places[1]
    shard = sum_v.shape[0] // 3
    last = places[2] - 1
    total = total_of(parts)
    row_part[...] = weighted(total[:shard], w_left)
    upper = when(z == 0, sum_v[:shard])
    lower = when(z == last, sum_v[2 * shard :])
    for to in range(out.shape[0]):
        out[to, :shard] = when(x - 1 == to, upper) + when(x + 1 == to, lower)
        out[to, shard:] = total[shard:]


def across_z_kernel(places, parts, sum_v, out):
    z = places[1]
    shard = sum_v.shape[0] // 3
    last = places[2] - 1
    total = total_of(parts)
    upper, lower = sum_v[:shard], sum_v[2 * shard :]
    crossed = total[:shard]
    for to in range(out.shape[0]):
        ends = jnp.logical_or(
            jnp.logical_and(z == 0, to == last), jnp.logical_and(z == last, to == 0)
        )
        out[to, :shard] = when(z - 1 == to, upper) + when(z + 1 == to, lower) + when(ends, crossed)
        out[to, shard:] = total[shard:]


def node_kernel(parts, sum_v, row_part, w_right, grad_nodes, shares):
    shard = sum_v.shape[0] // 3
    total = total_of(parts)
    columns = sum_v[shard : 2 * shard] + total[:shard]
    grad_nodes[...] = row_part[...] + weighted(columns, w_right)
    for chip in range(shares.shape[0]):
        shares[chip] = total[shard:].astype(shares.dtype)


def call(kernel, out_shape, *operands, scalars=1):
    specs = [SMEM] * scalars + [VMEM] * (len(operands) - scalars)
    return pl.pallas_call(
        kernel,
        out_shape=out_shape,
        in_specs=specs,
        out_specs=jax.tree.map(lambda _: VMEM, out_shape),
        compiler_params=PARAMS,
    )(*operands)


def split_kernel(core, own, other, left, right, harm, out, whole):
    chips, share = own.shape[0], own.shape[1]
    width = left.shape[0]
    for which, part in ((core[0], own), (1 - core[0], other)):
        for chip in range(chips):
            start = pl.multiple_of((which * chips + chip) * share, 8)
            whole[pl.ds(start, share), :] = part[chip].astype(F32)
    left[...] = whole[:width]
    right[...] = whole[width : 2 * width]
    at_out = 2 * width
    out[...] = whole[at_out : at_out + out.shape[0]]
    at_harm = at_out + OUT_ROWS
    harm[...] = whole[at_harm : at_harm + harm.shape[0]]


def split(core, own, other, harmonics, orbitals):
    chips, share, width = own.shape
    return pl.pallas_call(
        split_kernel,
        out_shape=(
            like(width, width), like(width, width), like(harmonics, width), like(orbitals, width),
        ),
        in_specs=[SMEM, VMEM, VMEM],
        out_specs=(VMEM,) * 4,
        scratch_shapes=[pltpu.VMEM((2 * chips * share, width), F32)],
        compiler_params=PARAMS,
    )(core, own, other)


def groups(size, bits):
    mask = sum(bits)
    found = {}
    for i in range(size):
        found.setdefault(i & ~mask, []).append(i)
    return list(found.values())


def exchange(blocks, axis, bits):
    return lax.all_to_all(
        blocks, axis, 0, 0, tiled=True, axis_index_groups=groups(lax.axis_size(axis), bits)
    )


def swapped(block):
    return lax.ppermute(block, "col", [(i, i ^ 1) for i in range(lax.axis_size("col"))])


def shifted(block, distance):
    devices = range(lax.axis_size("row"))
    return lax.ppermute(
        block, "row", [(i, i + distance) for i in devices if i + distance in devices]
    )


def repeated(block, copies):
    return jnp.broadcast_to(block[None], (copies,) + block.shape)


def body(
    nodes,
    harmonics,
    grad_blocks,
    pair_rows,
    pair_cols,
    pair_mask,
    block_counts,
    w_left,
    w_right,
    w_harm,
    w_out,
):
    shard, width = nodes.shape
    columns = lax.axis_size("col")
    chips = columns // 2
    share = 24
    spread = 4
    row = lax.axis_index("row")
    core = jnp.bitwise_and(lax.axis_index("col"), 1)
    column_nodes = jnp.concatenate([shifted(nodes, 1), nodes, shifted(nodes, -1)])
    row_nodes = exchange(repeated(nodes, columns), "col", COL_BITS).reshape(-1, width)
    places = jnp.stack([block_counts[0, 0], (row - 1) * shard, core]).astype(jnp.int32)
    keep, send, sum_v = pair_sums(
        places, pair_rows[0], pair_cols[0], pair_mask[0], harmonics[0], grad_blocks[0],
        row_nodes, column_nodes, (w_left, w_right, w_harm, w_out), chips, share,
    )
    parts = (keep + swapped(send)).astype(BF16)
    parts = exchange(parts, "col", CHIP_BITS)
    at = jnp.stack([row // spread, row % spread, jnp.int32(spread)]).astype(jnp.int32)
    chunks = like(spread, shard + share, width)
    row_part, parts = call(
        across_x_kernel, (like(shard, width), chunks), at, parts, sum_v, w_left
    )
    parts = exchange(parts, "row", X_BITS)
    parts = call(across_z_kernel, chunks, at, parts, sum_v)
    parts = exchange(parts, "row", Z_BITS)
    grad_nodes, shares = call(
        node_kernel,
        (like(shard, width), jax.ShapeDtypeStruct((chips, share, width), BF16)),
        parts, sum_v, row_part, w_right, scalars=0,
    )
    own_shares = exchange(shares, "col", CHIP_BITS)
    left, right, harm, out = split(
        core.reshape(1), own_shares, swapped(own_shares), w_harm.shape[0], w_out.shape[0]
    )
    return (grad_nodes, left, right, harm, out)


def solution(mesh):
    return jax.shard_map(
        body,
        mesh=mesh,
        in_specs=(
            P(BOTH, None),
            P("row", "col", None, None),
            P("row", "col", None, None),
            P("row", "col", None),
            P("row", "col", None),
            P("row", "col", None),
            P("row", "col"),
            P(),
            P(),
            P(),
            P(),
        ),
        out_specs=(P(BOTH, None), P(), P(), P(), P()),
        check_vma=False,
    )
```

```python
import jax
import jax.numpy as jnp
from jax import lax
from jax.experimental import pallas as pl
from jax.experimental.pallas import tpu as pltpu
from jax.sharding import PartitionSpec as P

F32, BF16 = jnp.float32, jnp.bfloat16
VMEM = pl.BlockSpec(memory_space=pltpu.VMEM)
SMEM = pl.BlockSpec(memory_space=pltpu.SMEM)
PARAMS = pltpu.CompilerParams(vmem_limit_bytes=48 * 1024 * 1024)
BOTH = ("row", "col")
BLOCKS_PER_STEP = 8
OUT_ROWS = 176
X_BITS, Z_BITS, CHIP_BITS, COL_BITS = (4, 8), (1, 2), (2, 4, 8, 16), (1, 2, 4, 8, 16)


def like(*shape):
    return jax.ShapeDtypeStruct(shape, F32)


def dot(a, b, da, db):
    return lax.dot_general(a, b, (((da,), (db,)), ((), ())), preferred_element_type=F32)


def halves(x):
    high = x.astype(BF16)
    return high, (x - high.astype(F32)).astype(BF16)


def pair_kernel(
    places, rows, cols, mask, harm, grads, row_nodes, column_nodes, w_left, w_right, w_harm, w_out,
    keep, send, sum_v, u_parts, v_parts, harm_t, out_t, sum_u, weights,
):
    count, column_base, core = places[0], places[1], places[2]
    width = w_left.shape[0]
    atoms, near = row_nodes.shape[0], column_nodes.shape[0]
    shard = near // 3
    pairs = BLOCKS_PER_STEP * mask.shape[1]
    orbitals, harmonics = w_out.shape[0], w_harm.shape[0]
    high, low = halves(dot(w_left[...], row_nodes[...], 0, 1))
    u_parts[:width] = high
    u_parts[width:] = low
    v_parts[...] = jnp.concatenate(halves(dot(w_right[...], column_nodes[...], 0, 1)), axis=1)
    harm_t[...] = w_harm[...].astype(F32).T.astype(BF16)
    out_t[...] = w_out[...].astype(F32).T.astype(BF16)
    for total in (sum_u, sum_v, weights):
        total[...] = jnp.zeros_like(total)
    at_out = 2 * width
    at_harm = at_out + OUT_ROWS

    def line(ref, first):
        return jnp.concatenate(
            [ref[pl.ds(first + k, 1), :] for k in range(BLOCKS_PER_STEP)], axis=1
        )

    def step(i, carry):
        first = BLOCKS_PER_STEP * i
        live = jnp.concatenate(
            [
                mask[pl.ds(first + k, 1), :] * (first + k < count).astype(jnp.int32)
                for k in range(BLOCKS_PER_STEP)
            ],
            axis=1,
        )
        g = jnp.concatenate([grads[first + k] for k in range(BLOCKS_PER_STEP)], axis=1)
        g = g * live.astype(F32).astype(BF16)
        h = jnp.concatenate([harm[first + k] for k in range(BLOCKS_PER_STEP)], axis=1)
        at_u = lax.broadcasted_iota(jnp.int32, (atoms, pairs), 0) == line(rows, first)
        at_v = lax.broadcasted_iota(jnp.int32, (near, pairs), 0) == line(cols, first) - column_base
        pick_u = at_u.astype(F32).astype(BF16)
        pick_v = at_v.astype(F32).astype(BF16)
        parts = dot(u_parts[...], pick_u, 1, 0)
        u = parts[:width] + parts[width:]
        v = dot(v_parts[...], jnp.concatenate([pick_v, pick_v]), 1, 0)
        e = dot(harm_t[...], h, 1, 0)
        gz = dot(out_t[...], g, 1, 0)
        uv = u * v
        weights[at_out : at_out + orbitals] += dot(g, (uv * e).astype(BF16), 1, 1)
        weights[at_harm : at_harm + harmonics] += dot(h, (gz * uv).astype(BF16), 1, 1)
        ge = gz * e
        high, low = halves(ge * v)
        sum_u[...] += dot(pick_u, high, 1, 1) + dot(pick_u, low, 1, 1)
        high, low = halves(ge * u)
        sum_v[...] += dot(pick_v, high, 1, 1) + dot(pick_v, low, 1, 1)
        return carry

    lax.fori_loop(0, lax.div(count + BLOCKS_PER_STEP - 1, BLOCKS_PER_STEP), step, 0)
    for at, nodes, sums in ((0, row_nodes, sum_u), (width, column_nodes, sum_v)):
        high, low = halves(sums[...])
        weights[at : at + width] = dot(nodes[...], high, 0, 0) + dot(nodes[...], low, 0, 0)
    chips, chunk = keep.shape[0], keep.shape[1]
    share = chunk - shard
    for chip in range(chips):
        for to, which in ((keep, core), (send, 1 - core)):
            start = pl.multiple_of((2 * chip + which) * shard, 8)
            to[chip, :shard] = sum_u[pl.ds(start, shard), :]
            start = pl.multiple_of((which * chips + chip) * share, 8)
            to[chip, shard:] = weights[pl.ds(start, share), :]


def pair_sums(places, rows, cols, mask, harm, grads, row_nodes, column_nodes, weights_in, chips, share):
    atoms, width = row_nodes.shape
    near = column_nodes.shape[0]
    chunk = near // 3 + share
    w_harm, w_out = weights_in[2:]
    return pl.pallas_call(
        pair_kernel,
        out_shape=(like(chips, chunk, width), like(chips, chunk, width), like(near, width)),
        in_specs=[SMEM] + [VMEM] * 11,
        out_specs=(VMEM,) * 3,
        scratch_shapes=[
            pltpu.VMEM((2 * width, atoms), BF16),
            pltpu.VMEM((width, 2 * near), BF16),
            pltpu.VMEM(w_harm.shape[::-1], BF16),
            pltpu.VMEM(w_out.shape[::-1], BF16),
            pltpu.VMEM((atoms, width), F32),
            pltpu.VMEM((2 * chips * share, width), F32),
        ],
        compiler_params=PARAMS,
    )(places, rows, cols, mask, harm, grads, row_nodes, column_nodes, *weights_in)


def total_of(parts):
    total = parts[0].astype(F32)
    for i in range(1, parts.shape[0]):
        total = total + parts[i].astype(F32)
    return total


def weighted(sums, weight):
    high, low = halves(sums)
    return dot(high, weight[...], 1, 1) + dot(low, weight[...], 1, 1)


def row_kernel(parts, sum_v, upper, w_left, w_right, nodes_part, out):
    shard = nodes_part.shape[0]
    total = total_of(parts)
    columns = sum_v[shard : 2 * shard] + upper[...]
    nodes_part[...] = weighted(total[:shard], w_left) + weighted(columns, w_right)
    for to in range(out.shape[0]):
        out[to] = total[shard:]


def sum_kernel(parts, sum_v, out, lower):
    shard = lower.shape[0]
    total = total_of(parts)
    for to in range(out.shape[0]):
        out[to] = total
    lower[...] = sum_v[2 * shard :]


def node_kernel(parts, lower, nodes_part, w_right, grad_nodes, shares):
    grad_nodes[...] = nodes_part[...] + weighted(lower[...], w_right)
    total = total_of(parts).astype(shares.dtype)
    for chip in range(shares.shape[0]):
        shares[chip] = total


def call(kernel, out_shape, *operands):
    return pl.pallas_call(
        kernel,
        out_shape=out_shape,
        in_specs=[VMEM] * len(operands),
        out_specs=jax.tree.map(lambda _: VMEM, out_shape),
        compiler_params=PARAMS,
    )(*operands)


def split_kernel(core, own, other, left, right, harm, out, whole):
    chips, share = own.shape[0], own.shape[1]
    width = left.shape[0]
    for which, part in ((core[0], own), (1 - core[0], other)):
        for chip in range(chips):
            start = pl.multiple_of((which * chips + chip) * share, 8)
            whole[pl.ds(start, share), :] = part[chip].astype(F32)
    left[...] = whole[:width]
    right[...] = whole[width : 2 * width]
    at_out = 2 * width
    out[...] = whole[at_out : at_out + out.shape[0]]
    at_harm = at_out + OUT_ROWS
    harm[...] = whole[at_harm : at_harm + harm.shape[0]]


def split(core, own, other, harmonics, orbitals):
    chips, share, width = own.shape
    return pl.pallas_call(
        split_kernel,
        out_shape=(
            like(width, width), like(width, width), like(harmonics, width), like(orbitals, width),
        ),
        in_specs=[SMEM, VMEM, VMEM],
        out_specs=(VMEM,) * 4,
        scratch_shapes=[pltpu.VMEM((2 * chips * share, width), F32)],
        compiler_params=PARAMS,
    )(core, own, other)


def groups(size, bits):
    mask = sum(bits)
    found = {}
    for i in range(size):
        found.setdefault(i & ~mask, []).append(i)
    return list(found.values())


def exchange(blocks, axis, bits):
    return lax.all_to_all(
        blocks, axis, 0, 0, tiled=True, axis_index_groups=groups(lax.axis_size(axis), bits)
    )


def swapped(block):
    return lax.ppermute(block, "col", [(i, i ^ 1) for i in range(lax.axis_size("col"))])


def shifted(block, distance):
    devices = range(lax.axis_size("row"))
    return lax.ppermute(
        block, "row", [(i, i + distance) for i in devices if i + distance in devices]
    )


def repeated(block, copies):
    return jnp.broadcast_to(block[None], (copies,) + block.shape)


def body(
    nodes,
    harmonics,
    grad_blocks,
    pair_rows,
    pair_cols,
    pair_mask,
    block_counts,
    w_left,
    w_right,
    w_harm,
    w_out,
):
    shard, width = nodes.shape
    columns = lax.axis_size("col")
    chips = columns // 2
    share = 24
    spread = 4
    row = lax.axis_index("row")
    core = jnp.bitwise_and(lax.axis_index("col"), 1)
    column_nodes = jnp.concatenate([shifted(nodes, 1), nodes, shifted(nodes, -1)])
    row_nodes = exchange(repeated(nodes, columns), "col", COL_BITS).reshape(-1, width)
    places = jnp.stack([block_counts[0, 0], (row - 1) * shard, core]).astype(jnp.int32)
    keep, send, sum_v = pair_sums(
        places, pair_rows[0], pair_cols[0], pair_mask[0], harmonics[0], grad_blocks[0],
        row_nodes, column_nodes, (w_left, w_right, w_harm, w_out), chips, share,
    )
    parts = (keep + swapped(send)).astype(BF16)
    upper = shifted(sum_v[:shard], -1)
    parts = exchange(parts, "col", CHIP_BITS)
    block, chunks = like(shard, width), like(spread, share, width)
    nodes_part, parts = call(
        row_kernel, (block, chunks), parts, sum_v, upper, w_left, w_right
    )
    parts = exchange(parts, "row", X_BITS)
    parts, lower = call(sum_kernel, (chunks, block), parts, sum_v)
    lower = shifted(lower, 1)
    parts = exchange(parts, "row", Z_BITS)
    grad_nodes, shares = call(
        node_kernel,
        (block, jax.ShapeDtypeStruct((chips, share, width), BF16)),
        parts, lower, nodes_part, w_right,
    )
    own_shares = exchange(shares, "col", CHIP_BITS)
    left, right, harm, out = split(
        core.reshape(1), own_shares, swapped(own_shares), w_harm.shape[0], w_out.shape[0]
    )
    return (grad_nodes, left, right, harm, out)


def solution(mesh):
    return jax.shard_map(
        body,
        mesh=mesh,
        in_specs=(
            P(BOTH, None),
            P("row", "col", None, None),
            P("row", "col", None, None),
            P("row", "col", None),
            P("row", "col", None),
            P("row", "col", None),
            P("row", "col"),
            P(),
            P(),
            P(),
            P(),
        ),
        out_specs=(P(BOTH, None), P(), P(), P(), P()),
        check_vma=False,
    )
```

```python
import jax
import jax.numpy as jnp
from jax import lax
from jax.experimental import pallas as pl
from jax.experimental.pallas import tpu as pltpu
from jax.sharding import PartitionSpec as P

F32, BF16 = jnp.float32, jnp.bfloat16
VMEM = pl.BlockSpec(memory_space=pltpu.VMEM)
SMEM = pl.BlockSpec(memory_space=pltpu.SMEM)
PARAMS = pltpu.CompilerParams(vmem_limit_bytes=48 * 1024 * 1024)
BOTH = ("row", "col")
BLOCKS_PER_STEP = 8
OUT_ROWS = 176
X_BITS, Z_BITS, CHIP_BITS = (4, 8), (1, 2), (2, 4, 8, 16)


def like(*shape):
    return jax.ShapeDtypeStruct(shape, F32)


def dot(a, b, da, db):
    return lax.dot_general(a, b, (((da,), (db,)), ((), ())), preferred_element_type=F32)


def halves(x):
    high = x.astype(BF16)
    return high, (x - high.astype(F32)).astype(BF16)


def pair_kernel(
    places, rows, cols, mask, harm, grads, own, other, column_nodes, v_parts, w_left, w_harm, w_out,
    keep, send, middle, ahead, passed, u_parts, harm_t, out_t, sum_u, sum_v, weights,
):
    count, column_base, core = places[0], places[1], places[2]
    width = w_left.shape[0]
    half, near = own.shape[0], column_nodes.shape[0]
    atoms = 2 * half
    shard = near // 3
    pairs = BLOCKS_PER_STEP * mask.shape[1]
    orbitals, harmonics = w_out.shape[0], w_harm.shape[0]
    for first, nodes in ((0, own), (half, other)):
        high, low = halves(dot(w_left[...], nodes[...], 0, 1))
        u_parts[:width, first : first + half] = high
        u_parts[width:, first : first + half] = low
    harm_t[...] = w_harm[...].astype(F32).T.astype(BF16)
    out_t[...] = w_out[...].astype(F32).T.astype(BF16)
    for total in (sum_u, sum_v, weights):
        total[...] = jnp.zeros_like(total)
    at_out = 2 * width
    at_harm = at_out + OUT_ROWS

    def line(ref, first):
        return jnp.concatenate(
            [ref[pl.ds(first + k, 1), :] for k in range(BLOCKS_PER_STEP)], axis=1
        )

    def step(i, carry):
        first = BLOCKS_PER_STEP * i
        live = jnp.concatenate(
            [
                mask[pl.ds(first + k, 1), :] * (first + k < count).astype(jnp.int32)
                for k in range(BLOCKS_PER_STEP)
            ],
            axis=1,
        )
        g = jnp.concatenate([grads[first + k] for k in range(BLOCKS_PER_STEP)], axis=1)
        g = g * live.astype(F32).astype(BF16)
        h = jnp.concatenate([harm[first + k] for k in range(BLOCKS_PER_STEP)], axis=1)
        atom = line(rows, first)
        owner = lax.div(atom, shard)
        place = lax.shift_right_logical(owner, 1) * shard + lax.rem(atom, shard)
        place = place + jnp.where(jnp.bitwise_and(owner, 1) == core, 0, half)
        at_u = lax.broadcasted_iota(jnp.int32, (atoms, pairs), 0) == place
        at_v = lax.broadcasted_iota(jnp.int32, (near, pairs), 0) == line(cols, first) - column_base
        pick_u = at_u.astype(F32).astype(BF16)
        pick_v = at_v.astype(F32).astype(BF16)
        parts = dot(u_parts[...], pick_u, 1, 0)
        u = parts[:width] + parts[width:]
        v = dot(v_parts[...], jnp.concatenate([pick_v, pick_v]), 1, 0)
        e = dot(harm_t[...], h, 1, 0)
        gz = dot(out_t[...], g, 1, 0)
        uv = u * v
        weights[at_out : at_out + orbitals] += dot(g, (uv * e).astype(BF16), 1, 1)
        weights[at_harm : at_harm + harmonics] += dot(h, (gz * uv).astype(BF16), 1, 1)
        ge = gz * e
        high, low = halves(ge * v)
        sum_u[...] += dot(pick_u, high, 1, 1) + dot(pick_u, low, 1, 1)
        high, low = halves(ge * u)
        sum_v[...] += dot(pick_v, high, 1, 1) + dot(pick_v, low, 1, 1)
        return carry

    lax.fori_loop(0, lax.div(count + BLOCKS_PER_STEP - 1, BLOCKS_PER_STEP), step, 0)
    for at, blocks in (
        (0, ((own, sum_u[:half]), (other, sum_u[half:]))),
        (width, ((column_nodes, sum_v[...]),)),
    ):
        total = jnp.zeros((width, width), F32)
        for nodes, sums in blocks:
            for part in halves(sums):
                total = total + dot(nodes[...], part, 0, 0)
        weights[at : at + width] = total
    chips, chunk = keep.shape[0], keep.shape[1]
    share = chunk - shard
    for chip in range(chips):
        for to, first, which in ((keep, 0, core), (send, half, 1 - core)):
            to[chip, :shard] = sum_u[first + chip * shard : first + (chip + 1) * shard]
            start = pl.multiple_of((which * chips + chip) * share, 8)
            to[chip, shard:] = weights[pl.ds(start, share), :]
    middle[...] = sum_v[shard : 2 * shard]
    ahead[...] = sum_v[pl.ds(pl.multiple_of(core * 2 * shard, 8), shard), :]
    passed[...] = sum_v[pl.ds(pl.multiple_of((1 - core) * 2 * shard, 8), shard), :]


def project_kernel(own, column_nodes, w_right, copy, v_parts):
    copy[...] = own[...]
    v_parts[...] = jnp.concatenate(halves(dot(w_right[...], column_nodes[...], 0, 1)), axis=1)


def pair_sums(places, rows, cols, mask, harm, grads, own, other, column_nodes, v_parts, weights_in, chips, share):
    half, width = own.shape
    near = column_nodes.shape[0]
    shard = near // 3
    chunks, block = like(chips, shard + share, width), like(shard, width)
    w_harm, w_out = weights_in[1:]
    return pl.pallas_call(
        pair_kernel,
        out_shape=(chunks, chunks, block, block, block),
        in_specs=[SMEM] + [VMEM] * 12,
        out_specs=(VMEM,) * 5,
        scratch_shapes=[
            pltpu.VMEM((2 * width, 2 * half), BF16),
            pltpu.VMEM(w_harm.shape[::-1], BF16),
            pltpu.VMEM(w_out.shape[::-1], BF16),
            pltpu.VMEM((2 * half, width), F32),
            pltpu.VMEM((near, width), F32),
            pltpu.VMEM((2 * chips * share, width), F32),
        ],
        compiler_params=PARAMS,
    )(places, rows, cols, mask, harm, grads, own, other, column_nodes, v_parts, *weights_in)


def total_of(parts):
    total = parts[0].astype(F32)
    for i in range(1, parts.shape[0]):
        total = total + parts[i].astype(F32)
    return total


def weighted(sums, weight):
    high, low = halves(sums)
    return dot(high, weight[...], 1, 1) + dot(low, weight[...], 1, 1)


def row_kernel(parts, w_left, row_part, out):
    shard = row_part.shape[0]
    total = total_of(parts)
    row_part[...] = weighted(total[:shard], w_left)
    for to in range(out.shape[0]):
        out[to] = total[shard:]


def sum_kernel(parts, out):
    total = total_of(parts)
    for to in range(out.shape[0]):
        out[to] = total


def node_kernel(parts, middle, here, there, row_part, w_right, grad_nodes, shares):
    columns = middle[...] + here[...] + there[...]
    grad_nodes[...] = row_part[...] + weighted(columns, w_right)
    total = total_of(parts).astype(shares.dtype)
    for chip in range(shares.shape[0]):
        shares[chip] = total


def call(kernel, out_shape, *operands):
    return pl.pallas_call(
        kernel,
        out_shape=out_shape,
        in_specs=[VMEM] * len(operands),
        out_specs=jax.tree.map(lambda _: VMEM, out_shape),
        compiler_params=PARAMS,
    )(*operands)


def split_kernel(core, own, other, left, right, harm, out, whole):
    chips, share = own.shape[0], own.shape[1]
    width = left.shape[0]
    for which, part in ((core[0], own), (1 - core[0], other)):
        for chip in range(chips):
            start = pl.multiple_of((which * chips + chip) * share, 8)
            whole[pl.ds(start, share), :] = part[chip].astype(F32)
    left[...] = whole[:width]
    right[...] = whole[width : 2 * width]
    at_out = 2 * width
    out[...] = whole[at_out : at_out + out.shape[0]]
    at_harm = at_out + OUT_ROWS
    harm[...] = whole[at_harm : at_harm + harm.shape[0]]


def split(core, own, other, harmonics, orbitals):
    chips, share, width = own.shape
    return pl.pallas_call(
        split_kernel,
        out_shape=(
            like(width, width), like(width, width), like(harmonics, width), like(orbitals, width),
        ),
        in_specs=[SMEM, VMEM, VMEM],
        out_specs=(VMEM,) * 4,
        scratch_shapes=[pltpu.VMEM((2 * chips * share, width), F32)],
        compiler_params=PARAMS,
    )(core, own, other)


def groups(size, bits):
    mask = sum(bits)
    found = {}
    for i in range(size):
        found.setdefault(i & ~mask, []).append(i)
    return list(found.values())


def exchange(blocks, axis, bits):
    return lax.all_to_all(
        blocks, axis, 0, 0, tiled=True, axis_index_groups=groups(lax.axis_size(axis), bits)
    )


def swapped(block):
    return lax.ppermute(block, "col", [(i, i ^ 1) for i in range(lax.axis_size("col"))])


def shifted(block, distance):
    devices = range(lax.axis_size("row"))
    return lax.ppermute(
        block, "row", [(i, i + distance) for i in devices if i + distance in devices]
    )


def neighbours(block):
    rows, columns = lax.axis_size("row"), lax.axis_size("col")
    route = []
    for row in range(rows):
        for column in range(columns):
            to = row + 2 * (column % 2) - 1
            if to in range(rows):
                route.append((row * columns + column, to * columns + column))
    return lax.ppermute(block, BOTH, route)


def repeated(block, copies):
    return jnp.broadcast_to(block[None], (copies,) + block.shape)


def body(
    nodes,
    harmonics,
    grad_blocks,
    pair_rows,
    pair_cols,
    pair_mask,
    block_counts,
    w_left,
    w_right,
    w_harm,
    w_out,
):
    shard, width = nodes.shape
    columns = lax.axis_size("col")
    chips = columns // 2
    share = 24
    spread = 4
    row = lax.axis_index("row")
    core = jnp.bitwise_and(lax.axis_index("col"), 1)
    column_nodes = jnp.concatenate([shifted(nodes, 1), nodes, shifted(nodes, -1)])
    own = exchange(repeated(nodes, chips), "col", CHIP_BITS).reshape(-1, width)
    own, v_parts = call(
        project_kernel,
        (
            jax.ShapeDtypeStruct(own.shape, BF16),
            jax.ShapeDtypeStruct((width, 2 * column_nodes.shape[0]), BF16),
        ),
        own, column_nodes, w_right,
    )
    other = swapped(own)
    places = jnp.stack([block_counts[0, 0], (row - 1) * shard, core]).astype(jnp.int32)
    keep, send, middle, ahead, passed = pair_sums(
        places, pair_rows[0], pair_cols[0], pair_mask[0], harmonics[0], grad_blocks[0],
        own, other, column_nodes, v_parts, (w_left, w_harm, w_out), chips, share,
    )
    parts = (keep + swapped(send)).astype(BF16)
    parts = exchange(parts, "col", CHIP_BITS)
    passed = swapped(passed)
    both = jnp.where(
        core == 0, jnp.concatenate([ahead, passed]), jnp.concatenate([passed, ahead])
    )
    both = neighbours(both)
    here = jnp.where(core == 0, both[:shard], both[shard:])
    there = swapped(jnp.where(core == 0, both[shard:], both[:shard]))
    row_part, parts = call(
        row_kernel, (like(shard, width), like(spread, share, width)), parts, w_left
    )
    parts = exchange(parts, "row", X_BITS)
    parts = call(sum_kernel, like(spread, share, width), parts)
    parts = exchange(parts, "row", Z_BITS)
    grad_nodes, shares = call(
        node_kernel,
        (like(shard, width), jax.ShapeDtypeStruct((chips, share, width), BF16)),
        parts, middle, here, there, row_part, w_right,
    )
    own_shares = exchange(shares, "col", CHIP_BITS)
    left, right, harm, out = split(
        core.reshape(1), own_shares, swapped(own_shares), w_harm.shape[0], w_out.shape[0]
    )
    return (grad_nodes, left, right, harm, out)


def solution(mesh):
    return jax.shard_map(
        body,
        mesh=mesh,
        in_specs=(
            P(BOTH, None),
            P("row", "col", None, None),
            P("row", "col", None, None),
            P("row", "col", None),
            P("row", "col", None),
            P("row", "col", None),
            P("row", "col"),
            P(),
            P(),
            P(),
            P(),
        ),
        out_specs=(P(BOTH, None), P(), P(), P(), P()),
        check_vma=False,
    )
```

```python
import jax
import jax.numpy as jnp
from jax import lax
from jax.experimental import pallas as pl
from jax.experimental.pallas import tpu as pltpu
from jax.sharding import PartitionSpec as P

F32, BF16 = jnp.float32, jnp.bfloat16
VMEM = pl.BlockSpec(memory_space=pltpu.VMEM)
SMEM = pl.BlockSpec(memory_space=pltpu.SMEM)
PARAMS = pltpu.CompilerParams(vmem_limit_bytes=32 * 1024 * 1024)
BOTH = ("row", "col")
BLOCKS_PER_STEP = 8
OUT_ROWS = 176
X_BITS, Z_BITS, CHIP_BITS, COL_BITS = (4, 8), (1, 2), (2, 4, 8, 16), (1, 2, 4, 8, 16)


def like(*shape):
    return jax.ShapeDtypeStruct(shape, F32)


def dot(a, b, da, db):
    return lax.dot_general(a, b, (((da,), (db,)), ((), ())), preferred_element_type=F32)


def halves(x):
    high = x.astype(BF16)
    return high, (x - high.astype(F32)).astype(BF16)


def line(ref, first):
    return jnp.concatenate([ref[pl.ds(first + k, 1), :] for k in range(BLOCKS_PER_STEP)], axis=1)


def beside(ref, first):
    return jnp.concatenate([ref[first + k] for k in range(BLOCKS_PER_STEP)], axis=1)


def masked(places, mask, grads, first):
    live = [
        mask[pl.ds(first + k, 1), :] * (first + k < places[0]).astype(jnp.int32)
        for k in range(BLOCKS_PER_STEP)
    ]
    return beside(grads, first) * jnp.concatenate(live, axis=1).astype(F32).astype(BF16)


def picks(line_of_pairs, atoms):
    shape = (atoms, line_of_pairs.shape[1])
    at = lax.broadcasted_iota(jnp.int32, shape, 0) == line_of_pairs
    return at.astype(F32).astype(BF16)


def steps_of(places):
    return lax.div(places[0] + BLOCKS_PER_STEP - 1, BLOCKS_PER_STEP)


def row_pair_kernel(
    places, rows, mask, harm, grads, row_nodes, nodes, w_left, w_harm, w_out,
    u_pairs, e_pairs, gz_pairs, same_nodes, u_parts, harm_t, out_t,
):
    same_nodes[...] = nodes[...]
    width = w_left.shape[0]
    high, low = halves(dot(w_left[...], row_nodes[...], 0, 1))
    u_parts[:width] = high
    u_parts[width:] = low
    harm_t[...] = w_harm[...].astype(F32).T.astype(BF16)
    out_t[...] = w_out[...].astype(F32).T.astype(BF16)

    def step(i, carry):
        first = BLOCKS_PER_STEP * i
        parts = dot(u_parts[...], picks(line(rows, first), row_nodes.shape[0]), 1, 0)
        u_pairs[i] = parts[:width] + parts[width:]
        e_pairs[i] = dot(harm_t[...], beside(harm, first), 1, 0)
        gz_pairs[i] = dot(out_t[...], masked(places, mask, grads, first), 1, 0)
        return carry

    lax.fori_loop(0, steps_of(places), step, 0)


def pair_kernel(
    places, rows, cols, mask, harm, grads, row_nodes, column_nodes, w_right,
    u_pairs, e_pairs, gz_pairs,
    keep, send, middle, ahead, passed, v_parts, sum_u, sum_v, weights,
):
    column_base, core = places[1], places[2]
    width = w_right.shape[0]
    atoms, near = row_nodes.shape[0], column_nodes.shape[0]
    shard = near // 3
    orbitals, harmonics = grads.shape[1], harm.shape[1]
    v_parts[...] = jnp.concatenate(halves(dot(w_right[...], column_nodes[...], 0, 1)), axis=1)
    for total in (sum_u, sum_v, weights):
        total[...] = jnp.zeros_like(total)
    at_out = 2 * width
    at_harm = at_out + OUT_ROWS

    def step(i, carry):
        first = BLOCKS_PER_STEP * i
        g = masked(places, mask, grads, first)
        h = beside(harm, first)
        pick_u = picks(line(rows, first), atoms)
        pick_v = picks(line(cols, first) - column_base, near)
        v = dot(v_parts[...], jnp.concatenate([pick_v, pick_v]), 1, 0)
        u, e, gz = u_pairs[i], e_pairs[i], gz_pairs[i]
        uv = u * v
        weights[at_out : at_out + orbitals] += dot(g, (uv * e).astype(BF16), 1, 1)
        weights[at_harm : at_harm + harmonics] += dot(h, (gz * uv).astype(BF16), 1, 1)
        ge = gz * e
        high, low = halves(ge * v)
        sum_u[...] += dot(pick_u, high, 1, 1) + dot(pick_u, low, 1, 1)
        high, low = halves(ge * u)
        sum_v[...] += dot(pick_v, high, 1, 1) + dot(pick_v, low, 1, 1)
        return carry

    lax.fori_loop(0, steps_of(places), step, 0)
    for at, nodes, sums in ((0, row_nodes, sum_u), (width, column_nodes, sum_v)):
        high, low = halves(sums[...])
        weights[at : at + width] = dot(nodes[...], high, 0, 0) + dot(nodes[...], low, 0, 0)
    chips, chunk = keep.shape[0], keep.shape[1]
    share = chunk - shard
    for chip in range(chips):
        for to, which in ((keep, core), (send, 1 - core)):
            start = pl.multiple_of((2 * chip + which) * shard, 8)
            to[chip, :shard] = sum_u[pl.ds(start, shard), :]
            start = pl.multiple_of((which * chips + chip) * share, 8)
            to[chip, shard:] = weights[pl.ds(start, share), :]
    middle[...] = sum_v[shard : 2 * shard]
    ahead[...] = sum_v[pl.ds(pl.multiple_of(core * 2 * shard, 8), shard), :]
    passed[...] = sum_v[pl.ds(pl.multiple_of((1 - core) * 2 * shard, 8), shard), :]


def row_pairs(places, rows, mask, harm, grads, row_nodes, nodes, w_left, w_harm, w_out):
    atoms, width = row_nodes.shape
    pairs = BLOCKS_PER_STEP * rows.shape[1]
    steps = rows.shape[0] // BLOCKS_PER_STEP
    per_pair = like(steps, width, pairs)
    flops = 2 * steps * pairs * width * (2 * atoms + w_harm.shape[0] + w_out.shape[0])
    return pl.pallas_call(
        row_pair_kernel,
        out_shape=(per_pair,) * 3 + (jax.ShapeDtypeStruct(nodes.shape, BF16),),
        in_specs=[SMEM] + [VMEM] * 9,
        out_specs=(VMEM,) * 4,
        scratch_shapes=[
            pltpu.VMEM((2 * width, atoms), BF16),
            pltpu.VMEM(w_harm.shape[::-1], BF16),
            pltpu.VMEM(w_out.shape[::-1], BF16),
        ],
        compiler_params=PARAMS,
        cost_estimate=pl.CostEstimate(flops=flops, bytes_accessed=8 << 20, transcendentals=0),
    )(places, rows, mask, harm, grads, row_nodes, nodes, w_left, w_harm, w_out)


def pair_sums(
    places, rows, cols, mask, harm, grads, row_nodes, column_nodes, w_right, per_pair, chips, share
):
    atoms, width = row_nodes.shape
    near = column_nodes.shape[0]
    chunks, block = like(chips, near // 3 + share, width), like(near // 3, width)
    return pl.pallas_call(
        pair_kernel,
        out_shape=(chunks,) * 2 + (block,) * 3,
        in_specs=[SMEM] + [VMEM] * 11,
        out_specs=(VMEM,) * 5,
        scratch_shapes=[
            pltpu.VMEM((width, 2 * near), BF16),
            pltpu.VMEM((atoms, width), F32),
            pltpu.VMEM((near, width), F32),
            pltpu.VMEM((2 * chips * share, width), F32),
        ],
        compiler_params=PARAMS,
    )(places, rows, cols, mask, harm, grads, row_nodes, column_nodes, w_right, *per_pair)


def total_of(parts):
    total = parts[0].astype(F32)
    for i in range(1, parts.shape[0]):
        total = total + parts[i].astype(F32)
    return total


def weighted(sums, weight):
    high, low = halves(sums)
    return dot(high, weight[...], 1, 1) + dot(low, weight[...], 1, 1)


def row_kernel(parts, w_left, row_part, out):
    shard = row_part.shape[0]
    total = total_of(parts)
    row_part[...] = weighted(total[:shard], w_left)
    for to in range(out.shape[0]):
        out[to] = total[shard:]


def sum_kernel(parts, out):
    total = total_of(parts)
    for to in range(out.shape[0]):
        out[to] = total


def node_kernel(parts, middle, here, there, row_part, w_right, grad_nodes, shares):
    columns = middle[...] + here[...] + there[...]
    grad_nodes[...] = row_part[...] + weighted(columns, w_right)
    total = total_of(parts).astype(shares.dtype)
    for chip in range(shares.shape[0]):
        shares[chip] = total


def call(kernel, out_shape, *operands):
    return pl.pallas_call(
        kernel,
        out_shape=out_shape,
        in_specs=[VMEM] * len(operands),
        out_specs=jax.tree.map(lambda _: VMEM, out_shape),
        compiler_params=PARAMS,
    )(*operands)


def split_kernel(core, own, other, left, right, harm, out, whole):
    chips, share = own.shape[0], own.shape[1]
    width = left.shape[0]
    for which, part in ((core[0], own), (1 - core[0], other)):
        for chip in range(chips):
            start = pl.multiple_of((which * chips + chip) * share, 8)
            whole[pl.ds(start, share), :] = part[chip].astype(F32)
    left[...] = whole[:width]
    right[...] = whole[width : 2 * width]
    at_out = 2 * width
    out[...] = whole[at_out : at_out + out.shape[0]]
    at_harm = at_out + OUT_ROWS
    harm[...] = whole[at_harm : at_harm + harm.shape[0]]


def split(core, own, other, harmonics, orbitals):
    chips, share, width = own.shape
    return pl.pallas_call(
        split_kernel,
        out_shape=(
            like(width, width), like(width, width), like(harmonics, width), like(orbitals, width),
        ),
        in_specs=[SMEM, VMEM, VMEM],
        out_specs=(VMEM,) * 4,
        scratch_shapes=[pltpu.VMEM((2 * chips * share, width), F32)],
        compiler_params=PARAMS,
    )(core, own, other)


def groups(size, bits):
    mask = sum(bits)
    found = {}
    for i in range(size):
        found.setdefault(i & ~mask, []).append(i)
    return list(found.values())


def exchange(blocks, axis, bits):
    return lax.all_to_all(
        blocks, axis, 0, 0, tiled=True, axis_index_groups=groups(lax.axis_size(axis), bits)
    )


def swapped(block):
    return lax.ppermute(block, "col", [(i, i ^ 1) for i in range(lax.axis_size("col"))])


def shifted(block, distance):
    devices = range(lax.axis_size("row"))
    return lax.ppermute(
        block, "row", [(i, i + distance) for i in devices if i + distance in devices]
    )


def neighbours(block):
    rows, columns = lax.axis_size("row"), lax.axis_size("col")
    route = []
    for row in range(rows):
        for column in range(columns):
            to = row + 2 * (column % 2) - 1
            if to in range(rows):
                route.append((row * columns + column, to * columns + column))
    return lax.ppermute(block, BOTH, route)


def repeat_kernel(block, out):
    for i in range(out.shape[0]):
        out[i] = block[...]


def repeated(block, copies):
    return call(repeat_kernel, jax.ShapeDtypeStruct((copies,) + block.shape, block.dtype), block)


def body(
    nodes,
    harmonics,
    grad_blocks,
    pair_rows,
    pair_cols,
    pair_mask,
    block_counts,
    w_left,
    w_right,
    w_harm,
    w_out,
):
    shard, width = nodes.shape
    columns = lax.axis_size("col")
    chips = columns // 2
    share = 24
    spread = 4
    row = lax.axis_index("row")
    core = jnp.bitwise_and(lax.axis_index("col"), 1)
    before, after = shifted(nodes, 1), shifted(nodes, -1)
    row_nodes = exchange(repeated(nodes, columns), "col", COL_BITS).reshape(-1, width)
    places = jnp.stack([block_counts[0, 0], (row - 1) * shard, core]).astype(jnp.int32)
    rows, cols, mask = pair_rows[0], pair_cols[0], pair_mask[0]
    harm, grads = harmonics[0], grad_blocks[0]
    *per_pair, same_nodes = row_pairs(
        places, rows, mask, harm, grads, row_nodes, nodes, w_left, w_harm, w_out
    )
    column_nodes = jnp.concatenate([before, same_nodes, after])
    keep, send, middle, ahead, passed = pair_sums(
        places, rows, cols, mask, harm, grads, row_nodes, column_nodes, w_right, per_pair,
        chips, share,
    )
    parts = (keep + swapped(send)).astype(BF16)
    parts = exchange(parts, "col", CHIP_BITS)
    passed = swapped(passed)
    both = jnp.where(
        core == 0, jnp.concatenate([ahead, passed]), jnp.concatenate([passed, ahead])
    )
    both = neighbours(both)
    here = jnp.where(core == 0, both[:shard], both[shard:])
    there = swapped(jnp.where(core == 0, both[shard:], both[:shard]))
    row_part, parts = call(
        row_kernel, (like(shard, width), like(spread, share, width)), parts, w_left
    )
    parts = exchange(parts, "row", X_BITS)
    parts = call(sum_kernel, like(spread, share, width), parts)
    parts = exchange(parts, "row", Z_BITS)
    grad_nodes, shares = call(
        node_kernel,
        (like(shard, width), jax.ShapeDtypeStruct((chips, share, width), BF16)),
        parts, middle, here, there, row_part, w_right,
    )
    own_shares = exchange(shares, "col", CHIP_BITS)
    left, right, harm, out = split(
        core.reshape(1), own_shares, swapped(own_shares), w_harm.shape[0], w_out.shape[0]
    )
    return (grad_nodes, left, right, harm, out)


def solution(mesh):
    return jax.shard_map(
        body,
        mesh=mesh,
        in_specs=(
            P(BOTH, None),
            P("row", "col", None, None),
            P("row", "col", None, None),
            P("row", "col", None),
            P("row", "col", None),
            P("row", "col", None),
            P("row", "col"),
            P(),
            P(),
            P(),
            P(),
        ),
        out_specs=(P(BOTH, None), P(), P(), P(), P()),
        check_vma=False,
    )
```

```python
import jax
import jax.numpy as jnp
from jax import lax
from jax.experimental import pallas as pl
from jax.experimental.pallas import tpu as pltpu
from jax.sharding import PartitionSpec as P

F32, BF16 = jnp.float32, jnp.bfloat16
VMEM = pl.BlockSpec(memory_space=pltpu.VMEM)
SMEM = pl.BlockSpec(memory_space=pltpu.SMEM)
PARAMS = pltpu.CompilerParams(vmem_limit_bytes=32 * 1024 * 1024)
BOTH = ("row", "col")
BLOCKS_PER_STEP = 8
OUT_ROWS = 176
X_BITS, Z_BITS, CHIP_BITS, COL_BITS = (4, 8), (1, 2), (2, 4, 8, 16), (1, 2, 4, 8, 16)


def like(*shape):
    return jax.ShapeDtypeStruct(shape, F32)


def dot(a, b, da, db):
    return lax.dot_general(a, b, (((da,), (db,)), ((), ())), preferred_element_type=F32)


def halves(x):
    high = x.astype(BF16)
    return high, (x - high.astype(F32)).astype(BF16)


def line(ref, first):
    return jnp.concatenate([ref[pl.ds(first + k, 1), :] for k in range(BLOCKS_PER_STEP)], axis=1)


def beside(ref, first):
    return jnp.concatenate([ref[first + k] for k in range(BLOCKS_PER_STEP)], axis=1)


def masked(places, mask, grads, first):
    live = [
        mask[pl.ds(first + k, 1), :] * (first + k < places[0]).astype(jnp.int32)
        for k in range(BLOCKS_PER_STEP)
    ]
    return beside(grads, first) * jnp.concatenate(live, axis=1).astype(F32).astype(BF16)


def picks(line_of_pairs, atoms):
    shape = (atoms, line_of_pairs.shape[1])
    at = lax.broadcasted_iota(jnp.int32, shape, 0) == line_of_pairs
    return at.astype(F32).astype(BF16)


def steps_of(places):
    return lax.div(places[0] + BLOCKS_PER_STEP - 1, BLOCKS_PER_STEP)


def row_pair_kernel(
    places, rows, mask, harm, grads, row_nodes, nodes, w_left, w_harm, w_out,
    u_pairs, e_pairs, gz_pairs, same_nodes, u_parts, harm_t, out_t,
):
    same_nodes[...] = nodes[...]
    width = w_left.shape[0]
    high, low = halves(dot(w_left[...], row_nodes[...], 0, 1))
    u_parts[:width] = high
    u_parts[width:] = low
    harm_t[...] = w_harm[...].astype(F32).T.astype(BF16)
    out_t[...] = w_out[...].astype(F32).T.astype(BF16)

    def step(i, carry):
        first = BLOCKS_PER_STEP * i
        parts = dot(u_parts[...], picks(line(rows, first), row_nodes.shape[0]), 1, 0)
        u_pairs[i] = parts[:width] + parts[width:]
        e_pairs[i] = dot(harm_t[...], beside(harm, first), 1, 0)
        gz_pairs[i] = dot(out_t[...], masked(places, mask, grads, first), 1, 0)
        return carry

    lax.fori_loop(0, steps_of(places), step, 0)


def pair_kernel(
    places, rows, cols, mask, harm, grads, row_nodes, column_nodes, w_right,
    u_pairs, e_pairs, gz_pairs,
    keep, send, middle, ahead, passed, v_parts, sum_u, sum_v, weights,
):
    column_base, core = places[1], places[2]
    width = w_right.shape[0]
    atoms, near = row_nodes.shape[0], column_nodes.shape[0]
    shard = near // 3
    orbitals, harmonics = grads.shape[1], harm.shape[1]
    v_parts[...] = jnp.concatenate(halves(dot(w_right[...], column_nodes[...], 0, 1)), axis=1)
    for total in (sum_u, sum_v, weights):
        total[...] = jnp.zeros_like(total)
    at_out = 2 * width
    at_harm = at_out + OUT_ROWS

    def step(i, carry):
        first = BLOCKS_PER_STEP * i
        g = masked(places, mask, grads, first)
        h = beside(harm, first)
        pick_u = picks(line(rows, first), atoms)
        pick_v = picks(line(cols, first) - column_base, near)
        v = dot(v_parts[...], jnp.concatenate([pick_v, pick_v]), 1, 0)
        u, e, gz = u_pairs[i], e_pairs[i], gz_pairs[i]
        uv = u * v
        weights[at_out : at_out + orbitals] += dot(g, (uv * e).astype(BF16), 1, 1)
        weights[at_harm : at_harm + harmonics] += dot(h, (gz * uv).astype(BF16), 1, 1)
        ge = gz * e
        high, low = halves(ge * v)
        sum_u[...] += dot(pick_u, high, 1, 1) + dot(pick_u, low, 1, 1)
        high, low = halves(ge * u)
        sum_v[...] += dot(pick_v, high, 1, 1) + dot(pick_v, low, 1, 1)
        return carry

    lax.fori_loop(0, steps_of(places), step, 0)
    for at, nodes, sums in ((0, row_nodes, sum_u), (width, column_nodes, sum_v)):
        high, low = halves(sums[...])
        weights[at : at + width] = dot(nodes[...], high, 0, 0) + dot(nodes[...], low, 0, 0)
    chips, chunk = keep.shape[0], keep.shape[1]
    share = chunk - shard
    for chip in range(chips):
        for to, which in ((keep, core), (send, 1 - core)):
            start = pl.multiple_of((2 * chip + which) * shard, 8)
            to[chip, :shard] = sum_u[pl.ds(start, shard), :]
            start = pl.multiple_of((which * chips + chip) * share, 8)
            to[chip, shard:] = weights[pl.ds(start, share), :]
    middle[...] = sum_v[shard : 2 * shard]
    ahead[...] = sum_v[pl.ds(pl.multiple_of(core * 2 * shard, 8), shard), :]
    passed[...] = sum_v[pl.ds(pl.multiple_of((1 - core) * 2 * shard, 8), shard), :]


def row_pairs(places, rows, mask, harm, grads, row_nodes, nodes, w_left, w_harm, w_out):
    atoms, width = row_nodes.shape
    pairs = BLOCKS_PER_STEP * rows.shape[1]
    steps = rows.shape[0] // BLOCKS_PER_STEP
    per_pair = like(steps, width, pairs)
    flops = 2 * steps * pairs * width * (2 * atoms + w_harm.shape[0] + w_out.shape[0])
    return pl.pallas_call(
        row_pair_kernel,
        out_shape=(per_pair,) * 3 + (jax.ShapeDtypeStruct(nodes.shape, BF16),),
        in_specs=[SMEM] + [VMEM] * 9,
        out_specs=(VMEM,) * 4,
        scratch_shapes=[
            pltpu.VMEM((2 * width, atoms), BF16),
            pltpu.VMEM(w_harm.shape[::-1], BF16),
            pltpu.VMEM(w_out.shape[::-1], BF16),
        ],
        compiler_params=PARAMS,
        cost_estimate=pl.CostEstimate(flops=flops, bytes_accessed=8 << 20, transcendentals=0),
    )(places, rows, mask, harm, grads, row_nodes, nodes, w_left, w_harm, w_out)


def pair_sums(
    places, rows, cols, mask, harm, grads, row_nodes, column_nodes, w_right, per_pair, chips, share
):
    atoms, width = row_nodes.shape
    near = column_nodes.shape[0]
    chunks, block = like(chips, near // 3 + share, width), like(near // 3, width)
    return pl.pallas_call(
        pair_kernel,
        out_shape=(chunks,) * 2 + (block,) * 3,
        in_specs=[SMEM] + [VMEM] * 11,
        out_specs=(VMEM,) * 5,
        scratch_shapes=[
            pltpu.VMEM((width, 2 * near), BF16),
            pltpu.VMEM((atoms, width), F32),
            pltpu.VMEM((near, width), F32),
            pltpu.VMEM((2 * chips * share, width), F32),
        ],
        compiler_params=PARAMS,
    )(places, rows, cols, mask, harm, grads, row_nodes, column_nodes, w_right, *per_pair)


def total_of(parts):
    total = parts[0].astype(F32)
    for i in range(1, parts.shape[0]):
        total = total + parts[i].astype(F32)
    return total


def weighted(sums, weight):
    high, low = halves(sums)
    return dot(high, weight[...], 1, 1) + dot(low, weight[...], 1, 1)


def row_kernel(parts, w_left, row_part, out):
    shard = row_part.shape[0]
    total = total_of(parts)
    row_part[...] = weighted(total[:shard], w_left)
    for to in range(out.shape[0]):
        out[to] = total[shard:]


def sum_kernel(parts, out):
    total = total_of(parts)
    for to in range(out.shape[0]):
        out[to] = total


def node_kernel(parts, middle, here, there, row_part, w_right, grad_nodes, shares):
    columns = middle[...] + here[...] + there[...]
    grad_nodes[...] = row_part[...] + weighted(columns, w_right)
    total = total_of(parts).astype(shares.dtype)
    for chip in range(shares.shape[0]):
        shares[chip] = total


def call(kernel, out_shape, *operands):
    return pl.pallas_call(
        kernel,
        out_shape=out_shape,
        in_specs=[VMEM] * len(operands),
        out_specs=jax.tree.map(lambda _: VMEM, out_shape),
        compiler_params=PARAMS,
    )(*operands)


def split_kernel(core, own, other, left, right, harm, out, whole):
    chips, share = own.shape[0], own.shape[1]
    width = left.shape[0]
    for which, part in ((core[0], own), (1 - core[0], other)):
        for chip in range(chips):
            start = pl.multiple_of((which * chips + chip) * share, 8)
            whole[pl.ds(start, share), :] = part[chip].astype(F32)
    left[...] = whole[:width]
    right[...] = whole[width : 2 * width]
    at_out = 2 * width
    out[...] = whole[at_out : at_out + out.shape[0]]
    at_harm = at_out + OUT_ROWS
    harm[...] = whole[at_harm : at_harm + harm.shape[0]]


def split(core, own, other, harmonics, orbitals):
    chips, share, width = own.shape
    return pl.pallas_call(
        split_kernel,
        out_shape=(
            like(width, width), like(width, width), like(harmonics, width), like(orbitals, width),
        ),
        in_specs=[SMEM, VMEM, VMEM],
        out_specs=(VMEM,) * 4,
        scratch_shapes=[pltpu.VMEM((2 * chips * share, width), F32)],
        compiler_params=PARAMS,
    )(core, own, other)


def groups(size, bits):
    mask = sum(bits)
    found = {}
    for i in range(size):
        found.setdefault(i & ~mask, []).append(i)
    return list(found.values())


def exchange(blocks, axis, bits):
    return lax.all_to_all(
        blocks, axis, 0, 0, tiled=True, axis_index_groups=groups(lax.axis_size(axis), bits)
    )


def crossed(blocks, bits):
    rows, columns = lax.axis_size("row"), lax.axis_size("col")
    found = {}
    for row in range(rows):
        for column in range(columns):
            key = (row & ~sum(bits[column % 2]), column)
            found.setdefault(key, []).append(row * columns + column)
    return lax.all_to_all(
        blocks, BOTH, 0, 0, tiled=True, axis_index_groups=list(found.values())
    )


def swapped(block):
    return lax.ppermute(block, "col", [(i, i ^ 1) for i in range(lax.axis_size("col"))])


def shifted(block, distance):
    devices = range(lax.axis_size("row"))
    return lax.ppermute(
        block, "row", [(i, i + distance) for i in devices if i + distance in devices]
    )


def neighbours(block):
    rows, columns = lax.axis_size("row"), lax.axis_size("col")
    route = []
    for row in range(rows):
        for column in range(columns):
            to = row + 2 * (column % 2) - 1
            if to in range(rows):
                route.append((row * columns + column, to * columns + column))
    return lax.ppermute(block, BOTH, route)


def repeat_kernel(block, out):
    for i in range(out.shape[0]):
        out[i] = block[...]


def repeated(block, copies):
    return call(repeat_kernel, jax.ShapeDtypeStruct((copies,) + block.shape, block.dtype), block)


def body(
    nodes,
    harmonics,
    grad_blocks,
    pair_rows,
    pair_cols,
    pair_mask,
    block_counts,
    w_left,
    w_right,
    w_harm,
    w_out,
):
    shard, width = nodes.shape
    columns = lax.axis_size("col")
    chips = columns // 2
    share = 24
    spread = 4
    row = lax.axis_index("row")
    core = jnp.bitwise_and(lax.axis_index("col"), 1)
    before, after = shifted(nodes, 1), shifted(nodes, -1)
    row_nodes = exchange(repeated(nodes, columns), "col", COL_BITS).reshape(-1, width)
    places = jnp.stack([block_counts[0, 0], (row - 1) * shard, core]).astype(jnp.int32)
    rows, cols, mask = pair_rows[0], pair_cols[0], pair_mask[0]
    harm, grads = harmonics[0], grad_blocks[0]
    *per_pair, same_nodes = row_pairs(
        places, rows, mask, harm, grads, row_nodes, nodes, w_left, w_harm, w_out
    )
    column_nodes = jnp.concatenate([before, same_nodes, after])
    keep, send, middle, ahead, passed = pair_sums(
        places, rows, cols, mask, harm, grads, row_nodes, column_nodes, w_right, per_pair,
        chips, share,
    )
    parts = (keep + swapped(send)).astype(BF16)
    parts = exchange(parts, "col", CHIP_BITS)
    passed = swapped(passed)
    both = jnp.where(
        core == 0, jnp.concatenate([ahead, passed]), jnp.concatenate([passed, ahead])
    )
    both = neighbours(both)
    here = jnp.where(core == 0, both[:shard], both[shard:])
    there = swapped(jnp.where(core == 0, both[shard:], both[:shard]))
    row_part, parts = call(
        row_kernel, (like(shard, width), like(spread, share, width)), parts, w_left
    )
    parts = crossed(parts, (X_BITS, Z_BITS))
    parts = call(sum_kernel, like(spread, share, width), parts)
    parts = crossed(parts, (Z_BITS, X_BITS))
    grad_nodes, shares = call(
        node_kernel,
        (like(shard, width), jax.ShapeDtypeStruct((chips, share, width), BF16)),
        parts, middle, here, there, row_part, w_right,
    )
    own_shares = exchange(shares, "col", CHIP_BITS)
    left, right, harm, out = split(
        core.reshape(1), own_shares, swapped(own_shares), w_harm.shape[0], w_out.shape[0]
    )
    return (grad_nodes, left, right, harm, out)


def solution(mesh):
    return jax.shard_map(
        body,
        mesh=mesh,
        in_specs=(
            P(BOTH, None),
            P("row", "col", None, None),
            P("row", "col", None, None),
            P("row", "col", None),
            P("row", "col", None),
            P("row", "col", None),
            P("row", "col"),
            P(),
            P(),
            P(),
            P(),
        ),
        out_specs=(P(BOTH, None), P(), P(), P(), P()),
        check_vma=False,
    )
```

```python
import jax
import jax.numpy as jnp
from jax import lax
from jax.experimental import pallas as pl
from jax.experimental.pallas import tpu as pltpu
from jax.sharding import PartitionSpec as P

F32, BF16 = jnp.float32, jnp.bfloat16
VMEM = pl.BlockSpec(memory_space=pltpu.VMEM)
SMEM = pl.BlockSpec(memory_space=pltpu.SMEM)
PARAMS = pltpu.CompilerParams(vmem_limit_bytes=32 * 1024 * 1024)
BOTH = ("row", "col")
BLOCKS_PER_STEP = 8
OUT_ROWS = 176
X_BITS, Z_BITS, CHIP_BITS, COL_BITS = (4, 8), (1, 2), (2, 4, 8, 16), (1, 2, 4, 8, 16)


def like(*shape):
    return jax.ShapeDtypeStruct(shape, F32)


def dot(a, b, da, db):
    return lax.dot_general(a, b, (((da,), (db,)), ((), ())), preferred_element_type=F32)


def halves(x):
    high = x.astype(BF16)
    return high, (x - high.astype(F32)).astype(BF16)


def line(ref, first):
    return jnp.concatenate([ref[pl.ds(first + k, 1), :] for k in range(BLOCKS_PER_STEP)], axis=1)


def beside(ref, first):
    return jnp.concatenate([ref[first + k] for k in range(BLOCKS_PER_STEP)], axis=1)


def masked(places, mask, grads, first):
    live = [
        mask[pl.ds(first + k, 1), :] * (first + k < places[0]).astype(jnp.int32)
        for k in range(BLOCKS_PER_STEP)
    ]
    return beside(grads, first) * jnp.concatenate(live, axis=1).astype(F32).astype(BF16)


def picks(line_of_pairs, atoms):
    shape = (atoms, line_of_pairs.shape[1])
    at = lax.broadcasted_iota(jnp.int32, shape, 0) == line_of_pairs
    return at.astype(F32).astype(BF16)


def steps_of(places):
    return lax.div(places[0] + BLOCKS_PER_STEP - 1, BLOCKS_PER_STEP)


def row_pair_kernel(
    places, rows, mask, harm, grads, row_nodes, nodes, w_left, w_harm, w_out,
    u_pairs, e_pairs, gz_pairs, same_nodes, u_parts, harm_t, out_t,
):
    same_nodes[...] = nodes[...]
    width = w_left.shape[0]
    high, low = halves(dot(w_left[...], row_nodes[...], 0, 1))
    u_parts[:width] = high
    u_parts[width:] = low
    harm_t[...] = w_harm[...].astype(F32).T.astype(BF16)
    out_t[...] = w_out[...].astype(F32).T.astype(BF16)

    def step(i, carry):
        first = BLOCKS_PER_STEP * i
        parts = dot(u_parts[...], picks(line(rows, first), row_nodes.shape[0]), 1, 0)
        u_pairs[i] = parts[:width] + parts[width:]
        e_pairs[i] = dot(harm_t[...], beside(harm, first), 1, 0)
        gz_pairs[i] = dot(out_t[...], masked(places, mask, grads, first), 1, 0)
        return carry

    lax.fori_loop(0, steps_of(places), step, 0)


def pair_kernel(
    places, rows, cols, mask, harm, grads, row_nodes, column_nodes, w_right,
    u_pairs, e_pairs, gz_pairs,
    keep, send, middle, ahead, passed, v_parts, sum_u, sum_v, weights,
):
    column_base, core = places[1], places[2]
    width = w_right.shape[0]
    atoms, near = row_nodes.shape[0], column_nodes.shape[0]
    shard = near // 3
    orbitals, harmonics = grads.shape[1], harm.shape[1]
    v_parts[...] = jnp.concatenate(halves(dot(w_right[...], column_nodes[...], 0, 1)), axis=1)
    for total in (sum_u, sum_v, weights):
        total[...] = jnp.zeros_like(total)
    at_out = 2 * width
    at_harm = at_out + OUT_ROWS

    def step(i, carry):
        first = BLOCKS_PER_STEP * i
        g = masked(places, mask, grads, first)
        h = beside(harm, first)
        pick_u = picks(line(rows, first), atoms)
        pick_v = picks(line(cols, first) - column_base, near)
        v = dot(v_parts[...], jnp.concatenate([pick_v, pick_v]), 1, 0)
        u, e, gz = u_pairs[i], e_pairs[i], gz_pairs[i]
        uv = u * v
        weights[at_out : at_out + orbitals] += dot(g, (uv * e).astype(BF16), 1, 1)
        weights[at_harm : at_harm + harmonics] += dot(h, (gz * uv).astype(BF16), 1, 1)
        ge = gz * e
        high, low = halves(ge * v)
        sum_u[...] += dot(pick_u, high, 1, 1) + dot(pick_u, low, 1, 1)
        high, low = halves(ge * u)
        sum_v[...] += dot(pick_v, high, 1, 1) + dot(pick_v, low, 1, 1)
        return carry

    lax.fori_loop(0, steps_of(places), step, 0)
    for at, nodes, sums in ((0, row_nodes, sum_u), (width, column_nodes, sum_v)):
        high, low = halves(sums[...])
        weights[at : at + width] = dot(nodes[...], high, 0, 0) + dot(nodes[...], low, 0, 0)
    chips, chunk = keep.shape[0], keep.shape[1]
    share = chunk - shard
    for chip in range(chips):
        for to, which in ((keep, core), (send, 1 - core)):
            start = pl.multiple_of((2 * chip + which) * shard, 8)
            to[chip, :shard] = sum_u[pl.ds(start, shard), :]
            start = pl.multiple_of((which * chips + chip) * share, 8)
            to[chip, shard:] = weights[pl.ds(start, share), :]
    middle[...] = sum_v[shard : 2 * shard]
    ahead[...] = sum_v[pl.ds(pl.multiple_of(core * 2 * shard, 8), shard), :]
    passed[...] = sum_v[pl.ds(pl.multiple_of((1 - core) * 2 * shard, 8), shard), :]


def row_pairs(places, rows, mask, harm, grads, row_nodes, nodes, w_left, w_harm, w_out):
    atoms, width = row_nodes.shape
    pairs = BLOCKS_PER_STEP * rows.shape[1]
    steps = rows.shape[0] // BLOCKS_PER_STEP
    per_pair = like(steps, width, pairs)
    flops = 2 * steps * pairs * width * (2 * atoms + w_harm.shape[0] + w_out.shape[0])
    return pl.pallas_call(
        row_pair_kernel,
        out_shape=(per_pair,) * 3 + (jax.ShapeDtypeStruct(nodes.shape, BF16),),
        in_specs=[SMEM] + [VMEM] * 9,
        out_specs=(VMEM,) * 4,
        scratch_shapes=[
            pltpu.VMEM((2 * width, atoms), BF16),
            pltpu.VMEM(w_harm.shape[::-1], BF16),
            pltpu.VMEM(w_out.shape[::-1], BF16),
        ],
        compiler_params=PARAMS,
        cost_estimate=pl.CostEstimate(flops=flops, bytes_accessed=8 << 20, transcendentals=0),
    )(places, rows, mask, harm, grads, row_nodes, nodes, w_left, w_harm, w_out)


def pair_sums(
    places, rows, cols, mask, harm, grads, row_nodes, column_nodes, w_right, per_pair, chips, share
):
    atoms, width = row_nodes.shape
    near = column_nodes.shape[0]
    chunks, block = like(chips, near // 3 + share, width), like(near // 3, width)
    return pl.pallas_call(
        pair_kernel,
        out_shape=(chunks,) * 2 + (block,) * 3,
        in_specs=[SMEM] + [VMEM] * 11,
        out_specs=(VMEM,) * 5,
        scratch_shapes=[
            pltpu.VMEM((width, 2 * near), BF16),
            pltpu.VMEM((atoms, width), F32),
            pltpu.VMEM((near, width), F32),
            pltpu.VMEM((2 * chips * share, width), F32),
        ],
        compiler_params=PARAMS,
    )(places, rows, cols, mask, harm, grads, row_nodes, column_nodes, w_right, *per_pair)


def total_of(parts):
    total = parts[0].astype(F32)
    for i in range(1, parts.shape[0]):
        total = total + parts[i].astype(F32)
    return total


def weighted(sums, weight):
    high, low = halves(sums)
    return dot(high, weight[...], 1, 1) + dot(low, weight[...], 1, 1)


def row_kernel(core, parts, ahead, passed, row_sums, out, both):
    shard = row_sums.shape[0]
    total = total_of(parts)
    row_sums[...] = total[:shard]
    for to in range(out.shape[0]):
        out[to] = total[shard:]
    first = core[0] == 0
    both[:shard] = jnp.where(first, ahead[...], passed[...])
    both[shard:] = jnp.where(first, passed[...], ahead[...])


def middle_kernel(parts, out):
    total = total_of(parts)
    for to in range(out.shape[0]):
        out[to] = total


def last_kernel(parts, middle, here, there, out, column_sums):
    total = total_of(parts).astype(out.dtype)
    for to in range(out.shape[0]):
        out[to] = total
    column_sums[...] = middle[...] + here[...] + there[...]


def node_kernel(row_sums, column_sums, w_left, w_right, grad_nodes):
    grad_nodes[...] = weighted(row_sums[...], w_left) + weighted(column_sums[...], w_right)


def call(kernel, out_shape, *operands, scalars=0):
    specs = [SMEM] * scalars + [VMEM] * (len(operands) - scalars)
    return pl.pallas_call(
        kernel,
        out_shape=out_shape,
        in_specs=specs,
        out_specs=jax.tree.map(lambda _: VMEM, out_shape),
        compiler_params=PARAMS,
    )(*operands)


def split_kernel(core, own, other, left, right, harm, out, whole):
    chips, share = own.shape[0], own.shape[1]
    width = left.shape[0]
    for which, part in ((core[0], own), (1 - core[0], other)):
        for chip in range(chips):
            start = pl.multiple_of((which * chips + chip) * share, 8)
            whole[pl.ds(start, share), :] = part[chip].astype(F32)
    left[...] = whole[:width]
    right[...] = whole[width : 2 * width]
    at_out = 2 * width
    out[...] = whole[at_out : at_out + out.shape[0]]
    at_harm = at_out + OUT_ROWS
    harm[...] = whole[at_harm : at_harm + harm.shape[0]]


def split(core, own, other, harmonics, orbitals):
    chips, share, width = own.shape
    return pl.pallas_call(
        split_kernel,
        out_shape=(
            like(width, width), like(width, width), like(harmonics, width), like(orbitals, width),
        ),
        in_specs=[SMEM, VMEM, VMEM],
        out_specs=(VMEM,) * 4,
        scratch_shapes=[pltpu.VMEM((2 * chips * share, width), F32)],
        compiler_params=PARAMS,
    )(core, own, other)


def groups(size, bits):
    mask = sum(bits)
    found = {}
    for i in range(size):
        found.setdefault(i & ~mask, []).append(i)
    return list(found.values())


def exchange(blocks, axis, bits):
    return lax.all_to_all(
        blocks, axis, 0, 0, tiled=True, axis_index_groups=groups(lax.axis_size(axis), bits)
    )


def swapped(block):
    return lax.ppermute(block, "col", [(i, i ^ 1) for i in range(lax.axis_size("col"))])


def shifted(block, distance):
    devices = range(lax.axis_size("row"))
    return lax.ppermute(
        block, "row", [(i, i + distance) for i in devices if i + distance in devices]
    )


def neighbours(block):
    rows, columns = lax.axis_size("row"), lax.axis_size("col")
    route = []
    for row in range(rows):
        for column in range(columns):
            to = row + 2 * (column % 2) - 1
            if to in range(rows):
                route.append((row * columns + column, to * columns + column))
    return lax.ppermute(block, BOTH, route)


def repeat_kernel(block, out):
    for i in range(out.shape[0]):
        out[i] = block[...]


def repeated(block, copies):
    return call(repeat_kernel, jax.ShapeDtypeStruct((copies,) + block.shape, block.dtype), block)


def body(
    nodes,
    harmonics,
    grad_blocks,
    pair_rows,
    pair_cols,
    pair_mask,
    block_counts,
    w_left,
    w_right,
    w_harm,
    w_out,
):
    shard, width = nodes.shape
    columns = lax.axis_size("col")
    chips = columns // 2
    share = 24
    spread = 4
    row = lax.axis_index("row")
    core = jnp.bitwise_and(lax.axis_index("col"), 1)
    before, after = shifted(nodes, 1), shifted(nodes, -1)
    row_nodes = exchange(repeated(nodes, columns), "col", COL_BITS).reshape(-1, width)
    places = jnp.stack([block_counts[0, 0], (row - 1) * shard, core]).astype(jnp.int32)
    rows, cols, mask = pair_rows[0], pair_cols[0], pair_mask[0]
    harm, grads = harmonics[0], grad_blocks[0]
    *per_pair, same_nodes = row_pairs(
        places, rows, mask, harm, grads, row_nodes, nodes, w_left, w_harm, w_out
    )
    column_nodes = jnp.concatenate([before, same_nodes, after])
    keep, send, middle, ahead, passed = pair_sums(
        places, rows, cols, mask, harm, grads, row_nodes, column_nodes, w_right, per_pair,
        chips, share,
    )
    parts = (keep + swapped(send)).astype(BF16)
    parts = exchange(parts, "col", CHIP_BITS)
    passed = swapped(passed)
    block, chunks = like(shard, width), like(spread, share, width)
    core = core.reshape(1)
    row_sums, parts, both = call(
        row_kernel, (block, chunks, like(2 * shard, width)), core, parts, ahead, passed, scalars=1
    )
    parts = exchange(parts, "row", X_BITS)
    both = neighbours(both)
    parts = call(middle_kernel, chunks, parts)
    parts = exchange(parts, "row", Z_BITS)
    first = core[0] == 0
    here = jnp.where(first, both[:shard], both[shard:])
    there = swapped(jnp.where(first, both[shard:], both[:shard]))
    shares, column_sums = call(
        last_kernel,
        (jax.ShapeDtypeStruct((chips, share, width), BF16), block),
        parts, middle, here, there,
    )
    grad_nodes = call(node_kernel, block, row_sums, column_sums, w_left, w_right)
    own_shares = exchange(shares, "col", CHIP_BITS)
    left, right, harm, out = split(
        core, own_shares, swapped(own_shares), w_harm.shape[0], w_out.shape[0]
    )
    return (grad_nodes, left, right, harm, out)


def solution(mesh):
    return jax.shard_map(
        body,
        mesh=mesh,
        in_specs=(
            P(BOTH, None),
            P("row", "col", None, None),
            P("row", "col", None, None),
            P("row", "col", None),
            P("row", "col", None),
            P("row", "col", None),
            P("row", "col"),
            P(),
            P(),
            P(),
            P(),
        ),
        out_specs=(P(BOTH, None), P(), P(), P(), P()),
        check_vma=False,
    )
```

```python
import jax
import jax.numpy as jnp
from jax import lax
from jax.experimental import pallas as pl
from jax.experimental.pallas import tpu as pltpu
from jax.sharding import PartitionSpec as P

F32, BF16 = jnp.float32, jnp.bfloat16
VMEM = pl.BlockSpec(memory_space=pltpu.VMEM)
SMEM = pl.BlockSpec(memory_space=pltpu.SMEM)
PARAMS = pltpu.CompilerParams(vmem_limit_bytes=32 * 1024 * 1024)
BOTH = ("row", "col")
BLOCKS_PER_STEP = 8
OUT_ROWS = 176
SHARD = 32
X_BITS, Z_BITS, CHIP_BITS = (4, 8), (1, 2), (2, 4, 8, 16)


def like(*shape):
    return jax.ShapeDtypeStruct(shape, F32)


def dot(a, b, da, db):
    return lax.dot_general(a, b, (((da,), (db,)), ((), ())), preferred_element_type=F32)


def halves(x):
    high = x.astype(BF16)
    return high, (x - high.astype(F32)).astype(BF16)


def line(ref, first):
    return jnp.concatenate([ref[pl.ds(first + k, 1), :] for k in range(BLOCKS_PER_STEP)], axis=1)


def beside(ref, first):
    return jnp.concatenate([ref[first + k] for k in range(BLOCKS_PER_STEP)], axis=1)


def masked(places, mask, grads, first):
    live = [
        mask[pl.ds(first + k, 1), :] * (first + k < places[0]).astype(jnp.int32)
        for k in range(BLOCKS_PER_STEP)
    ]
    return beside(grads, first) * jnp.concatenate(live, axis=1).astype(F32).astype(BF16)


def picks(line_of_pairs, atoms):
    shape = (atoms, line_of_pairs.shape[1])
    at = lax.broadcasted_iota(jnp.int32, shape, 0) == line_of_pairs
    return at.astype(F32).astype(BF16)


def steps_of(places):
    return lax.div(places[0] + BLOCKS_PER_STEP - 1, BLOCKS_PER_STEP)


def places_of(places, rows, first, shard, half):
    atom = line(rows, first)
    owner = lax.div(atom, shard)
    place = lax.shift_right_logical(owner, 1) * shard + lax.rem(atom, shard)
    return place + jnp.where(jnp.bitwise_and(owner, 1) == places[2], 0, half)


def project(w_left, nodes, u_parts):
    width = w_left.shape[0]
    high, low = halves(dot(w_left[...], nodes[...], 0, 1))
    u_parts[:width] = high
    u_parts[width:] = low


def gathered(u_parts, place):
    width = u_parts.shape[0] // 2
    parts = dot(u_parts[...], picks(place, u_parts.shape[1]), 1, 0)
    return parts[:width] + parts[width:]


def own_pair_kernel(
    places, rows, mask, harm, grads, own, w_left, w_harm, w_out,
    u_pairs, e_pairs, gz_pairs, u_parts, harm_t, out_t,
):
    half = own.shape[0]
    project(w_left, own, u_parts)
    harm_t[...] = w_harm[...].astype(F32).T.astype(BF16)
    out_t[...] = w_out[...].astype(F32).T.astype(BF16)

    def step(i, carry):
        first = BLOCKS_PER_STEP * i
        u_pairs[i] = gathered(u_parts, places_of(places, rows, first, SHARD, half))
        e_pairs[i] = dot(harm_t[...], beside(harm, first), 1, 0)
        gz_pairs[i] = dot(out_t[...], masked(places, mask, grads, first), 1, 0)
        return carry

    lax.fori_loop(0, steps_of(places), step, 0)


def other_pair_kernel(places, rows, other, nodes, w_left, u_pairs, same_nodes, u_parts):
    half = other.shape[0]
    same_nodes[...] = nodes[...]
    project(w_left, other, u_parts)

    def step(i, carry):
        place = places_of(places, rows, BLOCKS_PER_STEP * i, SHARD, half)
        u_pairs[i] = gathered(u_parts, place - half)
        return carry

    lax.fori_loop(0, steps_of(places), step, 0)


def pair_kernel(
    places, rows, cols, mask, harm, grads, own, other, column_nodes, w_right,
    u_pairs, other_u_pairs, e_pairs, gz_pairs,
    keep, send, middle, ahead, passed, v_parts, sum_u, sum_v, weights,
):
    column_base, core = places[1], places[2]
    width = w_right.shape[0]
    half, near = own.shape[0], column_nodes.shape[0]
    shard = near // 3
    orbitals, harmonics = grads.shape[1], harm.shape[1]
    v_parts[...] = jnp.concatenate(halves(dot(w_right[...], column_nodes[...], 0, 1)), axis=1)
    for total in (sum_u, sum_v, weights):
        total[...] = jnp.zeros_like(total)
    at_out = 2 * width
    at_harm = at_out + OUT_ROWS

    def step(i, carry):
        first = BLOCKS_PER_STEP * i
        g = masked(places, mask, grads, first)
        h = beside(harm, first)
        pick_u = picks(places_of(places, rows, first, shard, half), 2 * half)
        pick_v = picks(line(cols, first) - column_base, near)
        v = dot(v_parts[...], jnp.concatenate([pick_v, pick_v]), 1, 0)
        u, e, gz = u_pairs[i] + other_u_pairs[i], e_pairs[i], gz_pairs[i]
        uv = u * v
        weights[at_out : at_out + orbitals] += dot(g, (uv * e).astype(BF16), 1, 1)
        weights[at_harm : at_harm + harmonics] += dot(h, (gz * uv).astype(BF16), 1, 1)
        ge = gz * e
        high, low = halves(ge * v)
        sum_u[...] += dot(pick_u, high, 1, 1) + dot(pick_u, low, 1, 1)
        high, low = halves(ge * u)
        sum_v[...] += dot(pick_v, high, 1, 1) + dot(pick_v, low, 1, 1)
        return carry

    lax.fori_loop(0, steps_of(places), step, 0)
    for at, blocks in (
        (0, ((own, sum_u[:half]), (other, sum_u[half:]))),
        (width, ((column_nodes, sum_v[...]),)),
    ):
        total = jnp.zeros((width, width), F32)
        for nodes, sums in blocks:
            for part in halves(sums):
                total = total + dot(nodes[...], part, 0, 0)
        weights[at : at + width] = total
    chips, chunk = keep.shape[0], keep.shape[1]
    share = chunk - shard
    for chip in range(chips):
        for to, first, which in ((keep, 0, core), (send, half, 1 - core)):
            to[chip, :shard] = sum_u[first + chip * shard : first + (chip + 1) * shard]
            start = pl.multiple_of((which * chips + chip) * share, 8)
            to[chip, shard:] = weights[pl.ds(start, share), :]
    middle[...] = sum_v[shard : 2 * shard]
    ahead[...] = sum_v[pl.ds(pl.multiple_of(core * 2 * shard, 8), shard), :]
    passed[...] = sum_v[pl.ds(pl.multiple_of((1 - core) * 2 * shard, 8), shard), :]


def own_pairs(places, rows, mask, harm, grads, own, w_left, w_harm, w_out):
    half, width = own.shape
    pairs = BLOCKS_PER_STEP * rows.shape[1]
    steps = rows.shape[0] // BLOCKS_PER_STEP
    return pl.pallas_call(
        own_pair_kernel,
        out_shape=(like(steps, width, pairs),) * 3,
        in_specs=[SMEM] + [VMEM] * 8,
        out_specs=(VMEM,) * 3,
        scratch_shapes=[
            pltpu.VMEM((2 * width, half), BF16),
            pltpu.VMEM(w_harm.shape[::-1], BF16),
            pltpu.VMEM(w_out.shape[::-1], BF16),
        ],
        compiler_params=PARAMS,
        cost_estimate=pl.CostEstimate(flops=2 << 30, bytes_accessed=8 << 20, transcendentals=0),
    )(places, rows, mask, harm, grads, own, w_left, w_harm, w_out)


def other_pairs(places, rows, other, nodes, w_left):
    half, width = other.shape
    pairs = BLOCKS_PER_STEP * rows.shape[1]
    steps = rows.shape[0] // BLOCKS_PER_STEP
    return pl.pallas_call(
        other_pair_kernel,
        out_shape=(like(steps, width, pairs), jax.ShapeDtypeStruct(nodes.shape, BF16)),
        in_specs=[SMEM] + [VMEM] * 4,
        out_specs=(VMEM,) * 2,
        scratch_shapes=[pltpu.VMEM((2 * width, half), BF16)],
        compiler_params=PARAMS,
        cost_estimate=pl.CostEstimate(flops=2 << 30, bytes_accessed=4 << 20, transcendentals=0),
    )(places, rows, other, nodes, w_left)


def pair_sums(
    places, rows, cols, mask, harm, grads, own, other, column_nodes, w_right, per_pair, chips, share
):
    half, width = own.shape
    near = column_nodes.shape[0]
    chunks, block = like(chips, near // 3 + share, width), like(near // 3, width)
    return pl.pallas_call(
        pair_kernel,
        out_shape=(chunks,) * 2 + (block,) * 3,
        in_specs=[SMEM] + [VMEM] * 13,
        out_specs=(VMEM,) * 5,
        scratch_shapes=[
            pltpu.VMEM((width, 2 * near), BF16),
            pltpu.VMEM((2 * half, width), F32),
            pltpu.VMEM((near, width), F32),
            pltpu.VMEM((2 * chips * share, width), F32),
        ],
        compiler_params=PARAMS,
    )(places, rows, cols, mask, harm, grads, own, other, column_nodes, w_right, *per_pair)


def total_of(parts):
    total = parts[0].astype(F32)
    for i in range(1, parts.shape[0]):
        total = total + parts[i].astype(F32)
    return total


def weighted(sums, weight):
    high, low = halves(sums)
    return dot(high, weight[...], 1, 1) + dot(low, weight[...], 1, 1)


def row_kernel(core, parts, ahead, passed, row_sums, out, both):
    shard = row_sums.shape[0]
    total = total_of(parts)
    row_sums[...] = total[:shard]
    for to in range(out.shape[0]):
        out[to] = total[shard:]
    first = core[0] == 0
    both[:shard] = jnp.where(first, ahead[...], passed[...])
    both[shard:] = jnp.where(first, passed[...], ahead[...])


def middle_kernel(parts, out):
    total = total_of(parts)
    for to in range(out.shape[0]):
        out[to] = total


def last_kernel(parts, middle, here, there, out, column_sums):
    total = total_of(parts).astype(out.dtype)
    for to in range(out.shape[0]):
        out[to] = total
    column_sums[...] = middle[...] + here[...] + there[...]


def node_kernel(row_sums, column_sums, w_left, w_right, grad_nodes):
    grad_nodes[...] = weighted(row_sums[...], w_left) + weighted(column_sums[...], w_right)


def call(kernel, out_shape, *operands, scalars=0):
    specs = [SMEM] * scalars + [VMEM] * (len(operands) - scalars)
    return pl.pallas_call(
        kernel,
        out_shape=out_shape,
        in_specs=specs,
        out_specs=jax.tree.map(lambda _: VMEM, out_shape),
        compiler_params=PARAMS,
    )(*operands)


def split_kernel(core, own, other, left, right, harm, out, whole):
    chips, share = own.shape[0], own.shape[1]
    width = left.shape[0]
    for which, part in ((core[0], own), (1 - core[0], other)):
        for chip in range(chips):
            start = pl.multiple_of((which * chips + chip) * share, 8)
            whole[pl.ds(start, share), :] = part[chip].astype(F32)
    left[...] = whole[:width]
    right[...] = whole[width : 2 * width]
    at_out = 2 * width
    out[...] = whole[at_out : at_out + out.shape[0]]
    at_harm = at_out + OUT_ROWS
    harm[...] = whole[at_harm : at_harm + harm.shape[0]]


def split(core, own, other, harmonics, orbitals):
    chips, share, width = own.shape
    return pl.pallas_call(
        split_kernel,
        out_shape=(
            like(width, width), like(width, width), like(harmonics, width), like(orbitals, width),
        ),
        in_specs=[SMEM, VMEM, VMEM],
        out_specs=(VMEM,) * 4,
        scratch_shapes=[pltpu.VMEM((2 * chips * share, width), F32)],
        compiler_params=PARAMS,
    )(core, own, other)


def groups(size, bits):
    mask = sum(bits)
    found = {}
    for i in range(size):
        found.setdefault(i & ~mask, []).append(i)
    return list(found.values())


def exchange(blocks, axis, bits):
    return lax.all_to_all(
        blocks, axis, 0, 0, tiled=True, axis_index_groups=groups(lax.axis_size(axis), bits)
    )


def swapped(block):
    return lax.ppermute(block, "col", [(i, i ^ 1) for i in range(lax.axis_size("col"))])


def shifted(block, distance):
    devices = range(lax.axis_size("row"))
    return lax.ppermute(
        block, "row", [(i, i + distance) for i in devices if i + distance in devices]
    )


def neighbours(block):
    rows, columns = lax.axis_size("row"), lax.axis_size("col")
    route = []
    for row in range(rows):
        for column in range(columns):
            to = row + 2 * (column % 2) - 1
            if to in range(rows):
                route.append((row * columns + column, to * columns + column))
    return lax.ppermute(block, BOTH, route)


def repeat_kernel(block, out):
    for i in range(out.shape[0]):
        out[i] = block[...]


def repeated(block, copies):
    return call(repeat_kernel, jax.ShapeDtypeStruct((copies,) + block.shape, block.dtype), block)


def body(
    nodes,
    harmonics,
    grad_blocks,
    pair_rows,
    pair_cols,
    pair_mask,
    block_counts,
    w_left,
    w_right,
    w_harm,
    w_out,
):
    shard, width = nodes.shape
    chips = lax.axis_size("col") // 2
    share = 24
    spread = 4
    row = lax.axis_index("row")
    core = jnp.bitwise_and(lax.axis_index("col"), 1)
    before, after = shifted(nodes, 1), shifted(nodes, -1)
    own = exchange(repeated(nodes, chips), "col", CHIP_BITS).reshape(-1, width)
    other = swapped(own)
    places = jnp.stack([block_counts[0, 0], (row - 1) * shard, core]).astype(jnp.int32)
    rows, cols, mask = pair_rows[0], pair_cols[0], pair_mask[0]
    harm, grads = harmonics[0], grad_blocks[0]
    own_u, e_pairs, gz_pairs = own_pairs(
        places, rows, mask, harm, grads, own, w_left, w_harm, w_out
    )
    other_u, same_nodes = other_pairs(places, rows, other, nodes, w_left)
    column_nodes = jnp.concatenate([before, same_nodes, after])
    keep, send, middle, ahead, passed = pair_sums(
        places, rows, cols, mask, harm, grads, own, other, column_nodes, w_right,
        (own_u, other_u, e_pairs, gz_pairs), chips, share,
    )
    parts = (keep + swapped(send)).astype(BF16)
    parts = exchange(parts, "col", CHIP_BITS)
    passed = swapped(passed)
    block, chunks = like(shard, width), like(spread, share, width)
    core = core.reshape(1)
    row_sums, parts, both = call(
        row_kernel, (block, chunks, like(2 * shard, width)), core, parts, ahead, passed, scalars=1
    )
    parts = exchange(parts, "row", X_BITS)
    both = neighbours(both)
    parts = call(middle_kernel, chunks, parts)
    parts = exchange(parts, "row", Z_BITS)
    first = core[0] == 0
    here = jnp.where(first, both[:shard], both[shard:])
    there = swapped(jnp.where(first, both[shard:], both[:shard]))
    shares, column_sums = call(
        last_kernel,
        (jax.ShapeDtypeStruct((chips, share, width), BF16), block),
        parts, middle, here, there,
    )
    grad_nodes = call(node_kernel, block, row_sums, column_sums, w_left, w_right)
    own_shares = exchange(shares, "col", CHIP_BITS)
    left, right, harm, out = split(
        core, own_shares, swapped(own_shares), w_harm.shape[0], w_out.shape[0]
    )
    return (grad_nodes, left, right, harm, out)


def solution(mesh):
    return jax.shard_map(
        body,
        mesh=mesh,
        in_specs=(
            P(BOTH, None),
            P("row", "col", None, None),
            P("row", "col", None, None),
            P("row", "col", None),
            P("row", "col", None),
            P("row", "col", None),
            P("row", "col"),
            P(),
            P(),
            P(),
            P(),
        ),
        out_specs=(P(BOTH, None), P(), P(), P(), P()),
        check_vma=False,
    )
```

```python
import jax
import jax.numpy as jnp
from jax import lax
from jax.experimental import pallas as pl
from jax.experimental.pallas import tpu as pltpu
from jax.sharding import PartitionSpec as P

F32, BF16 = jnp.float32, jnp.bfloat16
VMEM = pl.BlockSpec(memory_space=pltpu.VMEM)
SMEM = pl.BlockSpec(memory_space=pltpu.SMEM)
PARAMS = pltpu.CompilerParams(vmem_limit_bytes=32 * 1024 * 1024)
BOTH = ("row", "col")
BLOCKS_PER_STEP = 8
OUT_ROWS = 176
X_BITS, Z_BITS, CHIP_BITS, COL_BITS = (4, 8), (1, 2), (2, 4, 8, 16), (1, 2, 4, 8, 16)


def like(*shape):
    return jax.ShapeDtypeStruct(shape, F32)


def dot(a, b, da, db):
    return lax.dot_general(a, b, (((da,), (db,)), ((), ())), preferred_element_type=F32)


def halves(x):
    high = x.astype(BF16)
    return high, (x - high.astype(F32)).astype(BF16)


def line(ref, first):
    return jnp.concatenate([ref[pl.ds(first + k, 1), :] for k in range(BLOCKS_PER_STEP)], axis=1)


def beside(ref, first):
    return jnp.concatenate([ref[first + k] for k in range(BLOCKS_PER_STEP)], axis=1)


def masked(places, mask, grads, first):
    live = [
        mask[pl.ds(first + k, 1), :] * (first + k < places[0]).astype(jnp.int32)
        for k in range(BLOCKS_PER_STEP)
    ]
    return beside(grads, first) * jnp.concatenate(live, axis=1).astype(F32).astype(BF16)


def picks(line_of_pairs, atoms):
    shape = (atoms, line_of_pairs.shape[1])
    at = lax.broadcasted_iota(jnp.int32, shape, 0) == line_of_pairs
    return at.astype(F32).astype(BF16)


def steps_of(places):
    return lax.div(places[0] + BLOCKS_PER_STEP - 1, BLOCKS_PER_STEP)


def row_pair_kernel(
    places, rows, mask, harm, grads, row_nodes, nodes, w_left, w_harm, w_out,
    u_pairs, e_pairs, gz_pairs, same_nodes, u_parts, harm_t, out_t,
):
    same_nodes[...] = nodes[...]
    width = w_left.shape[0]
    high, low = halves(dot(w_left[...], row_nodes[...], 0, 1))
    u_parts[:width] = high
    u_parts[width:] = low
    harm_t[...] = w_harm[...].astype(F32).T.astype(BF16)
    out_t[...] = w_out[...].astype(F32).T.astype(BF16)

    def step(i, carry):
        first = BLOCKS_PER_STEP * i
        parts = dot(u_parts[...], picks(line(rows, first), row_nodes.shape[0]), 1, 0)
        u_pairs[i] = parts[:width] + parts[width:]
        e_pairs[i] = dot(harm_t[...], beside(harm, first), 1, 0)
        gz_pairs[i] = dot(out_t[...], masked(places, mask, grads, first), 1, 0)
        return carry

    lax.fori_loop(0, steps_of(places), step, 0)


def pair_kernel(
    places, rows, cols, mask, harm, grads, row_nodes, column_nodes, w_right,
    u_pairs, e_pairs, gz_pairs,
    keep, send, middle, ahead, passed, v_parts, sum_u, sum_v, weights,
):
    column_base, core = places[1], places[2]
    width = w_right.shape[0]
    atoms, near = row_nodes.shape[0], column_nodes.shape[0]
    shard = near // 3
    orbitals, harmonics = grads.shape[1], harm.shape[1]
    v_parts[...] = jnp.concatenate(halves(dot(w_right[...], column_nodes[...], 0, 1)), axis=1)
    for total in (sum_u, sum_v, weights):
        total[...] = jnp.zeros_like(total)
    at_out = 2 * width
    at_harm = at_out + OUT_ROWS

    def step(i, carry):
        first = BLOCKS_PER_STEP * i
        g = masked(places, mask, grads, first)
        h = beside(harm, first)
        pick_u = picks(line(rows, first), atoms)
        pick_v = picks(line(cols, first) - column_base, near)
        v = dot(v_parts[...], jnp.concatenate([pick_v, pick_v]), 1, 0)
        u, e, gz = u_pairs[i], e_pairs[i], gz_pairs[i]
        uv = u * v
        weights[at_out : at_out + orbitals] += dot(g, (uv * e).astype(BF16), 1, 1)
        weights[at_harm : at_harm + harmonics] += dot(h, (gz * uv).astype(BF16), 1, 1)
        ge = gz * e
        high, low = halves(ge * v)
        sum_u[...] += dot(pick_u, high, 1, 1) + dot(pick_u, low, 1, 1)
        high, low = halves(ge * u)
        sum_v[...] += dot(pick_v, high, 1, 1) + dot(pick_v, low, 1, 1)
        return carry

    lax.fori_loop(0, steps_of(places), step, 0)
    for at, nodes, sums in ((0, row_nodes, sum_u), (width, column_nodes, sum_v)):
        high, low = halves(sums[...])
        weights[at : at + width] = dot(nodes[...], high, 0, 0) + dot(nodes[...], low, 0, 0)
    chips, chunk = keep.shape[0], keep.shape[1]
    share = chunk - shard
    for chip in range(chips):
        for to, which in ((keep, core), (send, 1 - core)):
            start = pl.multiple_of((2 * chip + which) * shard, 8)
            to[chip, :shard] = sum_u[pl.ds(start, shard), :]
            start = pl.multiple_of((which * chips + chip) * share, 8)
            to[chip, shard:] = weights[pl.ds(start, share), :]
    middle[...] = sum_v[shard : 2 * shard]
    ahead[...] = sum_v[pl.ds(pl.multiple_of(core * 2 * shard, 8), shard), :]
    passed[...] = sum_v[pl.ds(pl.multiple_of((1 - core) * 2 * shard, 8), shard), :]


def row_pairs(places, rows, mask, harm, grads, row_nodes, nodes, w_left, w_harm, w_out):
    atoms, width = row_nodes.shape
    pairs = BLOCKS_PER_STEP * rows.shape[1]
    steps = rows.shape[0] // BLOCKS_PER_STEP
    per_pair = like(steps, width, pairs)
    flops = 2 * steps * pairs * width * (2 * atoms + w_harm.shape[0] + w_out.shape[0])
    return pl.pallas_call(
        row_pair_kernel,
        out_shape=(per_pair,) * 3 + (jax.ShapeDtypeStruct(nodes.shape, BF16),),
        in_specs=[SMEM] + [VMEM] * 9,
        out_specs=(VMEM,) * 4,
        scratch_shapes=[
            pltpu.VMEM((2 * width, atoms), BF16),
            pltpu.VMEM(w_harm.shape[::-1], BF16),
            pltpu.VMEM(w_out.shape[::-1], BF16),
        ],
        compiler_params=PARAMS,
        cost_estimate=pl.CostEstimate(flops=flops, bytes_accessed=8 << 20, transcendentals=0),
    )(places, rows, mask, harm, grads, row_nodes, nodes, w_left, w_harm, w_out)


def pair_sums(
    places, rows, cols, mask, harm, grads, row_nodes, column_nodes, w_right, per_pair, chips, share
):
    atoms, width = row_nodes.shape
    near = column_nodes.shape[0]
    chunks, block = like(chips, near // 3 + share, width), like(near // 3, width)
    return pl.pallas_call(
        pair_kernel,
        out_shape=(chunks,) * 2 + (block,) * 3,
        in_specs=[SMEM] + [VMEM] * 11,
        out_specs=(VMEM,) * 5,
        scratch_shapes=[
            pltpu.VMEM((width, 2 * near), BF16),
            pltpu.VMEM((atoms, width), F32),
            pltpu.VMEM((near, width), F32),
            pltpu.VMEM((2 * chips * share, width), F32),
        ],
        compiler_params=PARAMS,
    )(places, rows, cols, mask, harm, grads, row_nodes, column_nodes, w_right, *per_pair)


def total_of(parts):
    total = parts[0].astype(F32)
    for i in range(1, parts.shape[0]):
        total = total + parts[i].astype(F32)
    return total


def weighted(sums, weight):
    high, low = halves(sums)
    return dot(high, weight[...], 1, 1) + dot(low, weight[...], 1, 1)


def row_kernel(core, parts, ahead, passed, row_sums, out, both):
    shard = row_sums.shape[0]
    total = total_of(parts)
    row_sums[...] = total[:shard]
    for to in range(out.shape[0]):
        out[to] = total[shard:]
    first = core[0] == 0
    both[:shard] = jnp.where(first, ahead[...], passed[...])
    both[shard:] = jnp.where(first, passed[...], ahead[...])


def middle_kernel(parts, out):
    total = total_of(parts)
    for to in range(out.shape[0]):
        out[to] = total


def last_kernel(parts, middle, here, there, out, column_sums):
    total = total_of(parts).astype(out.dtype)
    for to in range(out.shape[0]):
        out[to] = total
    column_sums[...] = middle[...] + here[...] + there[...]


def node_kernel(row_sums, column_sums, w_left, w_right, grad_nodes):
    grad_nodes[...] = weighted(row_sums[...], w_left) + weighted(column_sums[...], w_right)


def call(kernel, out_shape, *operands, scalars=0):
    specs = [SMEM] * scalars + [VMEM] * (len(operands) - scalars)
    return pl.pallas_call(
        kernel,
        out_shape=out_shape,
        in_specs=specs,
        out_specs=jax.tree.map(lambda _: VMEM, out_shape),
        compiler_params=PARAMS,
    )(*operands)


def split_kernel(core, own, other, left, right, harm, out, whole):
    chips, share = own.shape[0], own.shape[1]
    width = left.shape[0]
    for which, part in ((core[0], own), (1 - core[0], other)):
        for chip in range(chips):
            start = pl.multiple_of((which * chips + chip) * share, 8)
            whole[pl.ds(start, share), :] = part[chip].astype(F32)
    left[...] = whole[:width]
    right[...] = whole[width : 2 * width]
    at_out = 2 * width
    out[...] = whole[at_out : at_out + out.shape[0]]
    at_harm = at_out + OUT_ROWS
    harm[...] = whole[at_harm : at_harm + harm.shape[0]]


def split(core, own, other, harmonics, orbitals):
    chips, share, width = own.shape
    return pl.pallas_call(
        split_kernel,
        out_shape=(
            like(width, width), like(width, width), like(harmonics, width), like(orbitals, width),
        ),
        in_specs=[SMEM, VMEM, VMEM],
        out_specs=(VMEM,) * 4,
        scratch_shapes=[pltpu.VMEM((2 * chips * share, width), F32)],
        compiler_params=PARAMS,
    )(core, own, other)


def groups(size, bits):
    mask = sum(bits)
    found = {}
    for i in range(size):
        found.setdefault(i & ~mask, []).append(i)
    return list(found.values())


def exchange(blocks, axis, bits):
    return lax.all_to_all(
        blocks, axis, 0, 0, tiled=True, axis_index_groups=groups(lax.axis_size(axis), bits)
    )


def swapped(block):
    return lax.ppermute(block, "col", [(i, i ^ 1) for i in range(lax.axis_size("col"))])


def shifted(block, distance):
    devices = range(lax.axis_size("row"))
    return lax.ppermute(
        block, "row", [(i, i + distance) for i in devices if i + distance in devices]
    )


def neighbours(block):
    rows, columns = lax.axis_size("row"), lax.axis_size("col")
    route = []
    for row in range(rows):
        for column in range(columns):
            to = row + 2 * (column % 2) - 1
            if to in range(rows):
                route.append((row * columns + column, to * columns + column))
    return lax.ppermute(block, BOTH, route)


def repeat_kernel(block, out, sems):
    copies = [
        pltpu.make_async_copy(block, out.at[i], sems.at[i]) for i in range(out.shape[0])
    ]
    for copy in copies:
        copy.start()
    for copy in copies:
        copy.wait()


def repeated(block, copies):
    anywhere = pl.BlockSpec(memory_space=pl.ANY)
    return pl.pallas_call(
        repeat_kernel,
        out_shape=jax.ShapeDtypeStruct((copies,) + block.shape, block.dtype),
        in_specs=[anywhere],
        out_specs=anywhere,
        scratch_shapes=[pltpu.SemaphoreType.DMA((copies,))],
        compiler_params=PARAMS,
    )(block)


def body(
    nodes,
    harmonics,
    grad_blocks,
    pair_rows,
    pair_cols,
    pair_mask,
    block_counts,
    w_left,
    w_right,
    w_harm,
    w_out,
):
    shard, width = nodes.shape
    columns = lax.axis_size("col")
    chips = columns // 2
    share = 24
    spread = 4
    row = lax.axis_index("row")
    core = jnp.bitwise_and(lax.axis_index("col"), 1)
    before, after = shifted(nodes, 1), shifted(nodes, -1)
    row_nodes = exchange(repeated(nodes, columns), "col", COL_BITS).reshape(-1, width)
    places = jnp.stack([block_counts[0, 0], (row - 1) * shard, core]).astype(jnp.int32)
    rows, cols, mask = pair_rows[0], pair_cols[0], pair_mask[0]
    harm, grads = harmonics[0], grad_blocks[0]
    *per_pair, same_nodes = row_pairs(
        places, rows, mask, harm, grads, row_nodes, nodes, w_left, w_harm, w_out
    )
    column_nodes = jnp.concatenate([before, same_nodes, after])
    keep, send, middle, ahead, passed = pair_sums(
        places, rows, cols, mask, harm, grads, row_nodes, column_nodes, w_right, per_pair,
        chips, share,
    )
    parts = (keep + swapped(send)).astype(BF16)
    parts = exchange(parts, "col", CHIP_BITS)
    passed = swapped(passed)
    block, chunks = like(shard, width), like(spread, share, width)
    core = core.reshape(1)
    row_sums, parts, both = call(
        row_kernel, (block, chunks, like(2 * shard, width)), core, parts, ahead, passed, scalars=1
    )
    parts = exchange(parts, "row", X_BITS)
    both = neighbours(both)
    parts = call(middle_kernel, chunks, parts)
    parts = exchange(parts, "row", Z_BITS)
    first = core[0] == 0
    here = jnp.where(first, both[:shard], both[shard:])
    there = swapped(jnp.where(first, both[shard:], both[:shard]))
    shares, column_sums = call(
        last_kernel,
        (jax.ShapeDtypeStruct((chips, share, width), BF16), block),
        parts, middle, here, there,
    )
    grad_nodes = call(node_kernel, block, row_sums, column_sums, w_left, w_right)
    own_shares = exchange(shares, "col", CHIP_BITS)
    left, right, harm, out = split(
        core, own_shares, swapped(own_shares), w_harm.shape[0], w_out.shape[0]
    )
    return (grad_nodes, left, right, harm, out)


def solution(mesh):
    return jax.shard_map(
        body,
        mesh=mesh,
        in_specs=(
            P(BOTH, None),
            P("row", "col", None, None),
            P("row", "col", None, None),
            P("row", "col", None),
            P("row", "col", None),
            P("row", "col", None),
            P("row", "col"),
            P(),
            P(),
            P(),
            P(),
        ),
        out_specs=(P(BOTH, None), P(), P(), P(), P()),
        check_vma=False,
    )
```

```python
import jax
import jax.numpy as jnp
from jax import lax
from jax.experimental import pallas as pl
from jax.experimental.pallas import tpu as pltpu
from jax.sharding import PartitionSpec as P

F32, BF16 = jnp.float32, jnp.bfloat16
VMEM = pl.BlockSpec(memory_space=pltpu.VMEM)
SMEM = pl.BlockSpec(memory_space=pltpu.SMEM)
PARAMS = pltpu.CompilerParams(vmem_limit_bytes=32 * 1024 * 1024)
BOTH = ("row", "col")
BLOCKS_PER_STEP = 8
OUT_ROWS = 176
X_BITS, Z_BITS, CHIP_BITS, COL_BITS = (4, 8), (1, 2), (2, 4, 8, 16), (1, 2, 4, 8, 16)


def like(*shape):
    return jax.ShapeDtypeStruct(shape, F32)


def dot(a, b, da, db):
    return lax.dot_general(a, b, (((da,), (db,)), ((), ())), preferred_element_type=F32)


def halves(x):
    high = x.astype(BF16)
    return high, (x - high.astype(F32)).astype(BF16)


def line(ref, first):
    return jnp.concatenate([ref[pl.ds(first + k, 1), :] for k in range(BLOCKS_PER_STEP)], axis=1)


def beside(ref, first):
    return jnp.concatenate([ref[first + k] for k in range(BLOCKS_PER_STEP)], axis=1)


def masked(places, mask, grads, first):
    live = [
        mask[pl.ds(first + k, 1), :] * (first + k < places[0]).astype(jnp.int32)
        for k in range(BLOCKS_PER_STEP)
    ]
    return beside(grads, first) * jnp.concatenate(live, axis=1).astype(F32).astype(BF16)


def picks(line_of_pairs, atoms):
    shape = (atoms, line_of_pairs.shape[1])
    at = lax.broadcasted_iota(jnp.int32, shape, 0) == line_of_pairs
    return at.astype(F32).astype(BF16)


def steps_of(places):
    return lax.div(places[0] + BLOCKS_PER_STEP - 1, BLOCKS_PER_STEP)


def row_pair_kernel(
    places, rows, mask, harm, grads, row_nodes, nodes, w_left, w_harm, w_out,
    u_pairs, e_pairs, gz_pairs, same_nodes, u_parts, harm_t, out_t,
):
    same_nodes[...] = nodes[...]
    width = w_left.shape[0]
    high, low = halves(dot(w_left[...], row_nodes[...], 0, 1))
    u_parts[:width] = high
    u_parts[width:] = low
    harm_t[...] = w_harm[...].astype(F32).T.astype(BF16)
    out_t[...] = w_out[...].astype(F32).T.astype(BF16)

    def step(i, carry):
        first = BLOCKS_PER_STEP * i
        parts = dot(u_parts[...], picks(line(rows, first), row_nodes.shape[0]), 1, 0)
        u_pairs[i] = parts[:width] + parts[width:]
        e_pairs[i] = dot(harm_t[...], beside(harm, first), 1, 0)
        gz_pairs[i] = dot(out_t[...], masked(places, mask, grads, first), 1, 0)
        return carry

    lax.fori_loop(0, steps_of(places), step, 0)


def pair_kernel(
    places, rows, cols, mask, harm, grads, row_nodes, column_nodes, w_right,
    u_pairs, e_pairs, gz_pairs,
    keep, send, middle, ahead, passed, v_parts, sum_u, sum_v, weights,
):
    column_base, core = places[1], places[2]
    width = w_right.shape[0]
    atoms, near = row_nodes.shape[0], column_nodes.shape[0]
    shard = near // 3
    orbitals, harmonics = grads.shape[1], harm.shape[1]
    v_parts[...] = jnp.concatenate(halves(dot(w_right[...], column_nodes[...], 0, 1)), axis=1)
    for total in (sum_u, sum_v, weights):
        total[...] = jnp.zeros_like(total)
    at_out = 2 * width
    at_harm = at_out + OUT_ROWS

    def step(i, carry):
        first = BLOCKS_PER_STEP * i
        g = masked(places, mask, grads, first)
        h = beside(harm, first)
        pick_u = picks(line(rows, first), atoms)
        pick_v = picks(line(cols, first) - column_base, near)
        v = dot(v_parts[...], jnp.concatenate([pick_v, pick_v]), 1, 0)
        u, e, gz = u_pairs[i], e_pairs[i], gz_pairs[i]
        uv = u * v
        weights[at_out : at_out + orbitals] += dot(g, (uv * e).astype(BF16), 1, 1)
        weights[at_harm : at_harm + harmonics] += dot(h, (gz * uv).astype(BF16), 1, 1)
        ge = gz * e
        high, low = halves(ge * v)
        sum_u[...] += dot(pick_u, high, 1, 1) + dot(pick_u, low, 1, 1)
        high, low = halves(ge * u)
        sum_v[...] += dot(pick_v, high, 1, 1) + dot(pick_v, low, 1, 1)
        return carry

    lax.fori_loop(0, steps_of(places), step, 0)
    for at, nodes, sums in ((0, row_nodes, sum_u), (width, column_nodes, sum_v)):
        high, low = halves(sums[...])
        weights[at : at + width] = dot(nodes[...], high, 0, 0) + dot(nodes[...], low, 0, 0)
    chips, chunk = keep.shape[0], keep.shape[1]
    share = chunk - shard
    for chip in range(chips):
        for to, which in ((keep, core), (send, 1 - core)):
            start = pl.multiple_of((2 * chip + which) * shard, 8)
            to[chip, :shard] = sum_u[pl.ds(start, shard), :]
            start = pl.multiple_of((which * chips + chip) * share, 8)
            to[chip, shard:] = weights[pl.ds(start, share), :]
    middle[...] = sum_v[shard : 2 * shard]
    ahead[...] = sum_v[pl.ds(pl.multiple_of(core * 2 * shard, 8), shard), :]
    passed[...] = sum_v[pl.ds(pl.multiple_of((1 - core) * 2 * shard, 8), shard), :]


def row_pairs(places, rows, mask, harm, grads, row_nodes, nodes, w_left, w_harm, w_out):
    atoms, width = row_nodes.shape
    pairs = BLOCKS_PER_STEP * rows.shape[1]
    steps = rows.shape[0] // BLOCKS_PER_STEP
    per_pair = like(steps, width, pairs)
    flops = 2 * steps * pairs * width * (2 * atoms + w_harm.shape[0] + w_out.shape[0])
    return pl.pallas_call(
        row_pair_kernel,
        out_shape=(per_pair,) * 3 + (jax.ShapeDtypeStruct(nodes.shape, BF16),),
        in_specs=[SMEM] + [VMEM] * 9,
        out_specs=(VMEM,) * 4,
        scratch_shapes=[
            pltpu.VMEM((2 * width, atoms), BF16),
            pltpu.VMEM(w_harm.shape[::-1], BF16),
            pltpu.VMEM(w_out.shape[::-1], BF16),
        ],
        compiler_params=PARAMS,
        cost_estimate=pl.CostEstimate(flops=flops, bytes_accessed=8 << 20, transcendentals=0),
    )(places, rows, mask, harm, grads, row_nodes, nodes, w_left, w_harm, w_out)


def pair_sums(
    places, rows, cols, mask, harm, grads, row_nodes, column_nodes, w_right, per_pair, chips, share
):
    atoms, width = row_nodes.shape
    near = column_nodes.shape[0]
    chunks, block = like(chips, near // 3 + share, width), like(near // 3, width)
    return pl.pallas_call(
        pair_kernel,
        out_shape=(chunks,) * 2 + (block,) * 3,
        in_specs=[SMEM] + [VMEM] * 11,
        out_specs=(VMEM,) * 5,
        scratch_shapes=[
            pltpu.VMEM((width, 2 * near), BF16),
            pltpu.VMEM((atoms, width), F32),
            pltpu.VMEM((near, width), F32),
            pltpu.VMEM((2 * chips * share, width), F32),
        ],
        compiler_params=PARAMS,
    )(places, rows, cols, mask, harm, grads, row_nodes, column_nodes, w_right, *per_pair)


def total_of(parts):
    total = parts[0].astype(F32)
    for i in range(1, parts.shape[0]):
        total = total + parts[i].astype(F32)
    return total


def weighted(sums, weight):
    high, low = halves(sums)
    return dot(high, weight[...], 1, 1) + dot(low, weight[...], 1, 1)


def row_kernel(core, parts, ahead, passed, row_sums, out, both):
    shard = row_sums.shape[0]
    total = total_of(parts)
    row_sums[...] = total[:shard]
    for to in range(out.shape[0]):
        out[to] = total[shard:]
    first = core[0] == 0
    both[:shard] = jnp.where(first, ahead[...], passed[...])
    both[shard:] = jnp.where(first, passed[...], ahead[...])


def middle_kernel(parts, out):
    total = total_of(parts)
    for to in range(out.shape[0]):
        out[to] = total


def last_kernel(parts, middle, here, there, out, column_sums):
    total = total_of(parts).astype(out.dtype)
    for to in range(out.shape[0]):
        out[to] = total
    column_sums[...] = middle[...] + here[...] + there[...]


def node_kernel(row_sums, column_sums, w_left, w_right, grad_nodes):
    grad_nodes[...] = weighted(row_sums[...], w_left) + weighted(column_sums[...], w_right)


def call(kernel, out_shape, *operands, scalars=0):
    specs = [SMEM] * scalars + [VMEM] * (len(operands) - scalars)
    return pl.pallas_call(
        kernel,
        out_shape=out_shape,
        in_specs=specs,
        out_specs=jax.tree.map(lambda _: VMEM, out_shape),
        compiler_params=PARAMS,
    )(*operands)


def split_kernel(core, own, other, left, right, harm, out, whole):
    chips, share = own.shape[0], own.shape[1]
    width = left.shape[0]
    for which, part in ((core[0], own), (1 - core[0], other)):
        for chip in range(chips):
            start = pl.multiple_of((which * chips + chip) * share, 8)
            whole[pl.ds(start, share), :] = part[chip].astype(F32)
    left[...] = whole[:width]
    right[...] = whole[width : 2 * width]
    at_out = 2 * width
    out[...] = whole[at_out : at_out + out.shape[0]]
    at_harm = at_out + OUT_ROWS
    harm[...] = whole[at_harm : at_harm + harm.shape[0]]


def split(core, own, other, harmonics, orbitals):
    chips, share, width = own.shape
    return pl.pallas_call(
        split_kernel,
        out_shape=(
            like(width, width), like(width, width), like(harmonics, width), like(orbitals, width),
        ),
        in_specs=[SMEM, VMEM, VMEM],
        out_specs=(VMEM,) * 4,
        scratch_shapes=[pltpu.VMEM((2 * chips * share, width), F32)],
        compiler_params=PARAMS,
    )(core, own, other)


def groups(size, bits):
    mask = sum(bits)
    found = {}
    for i in range(size):
        found.setdefault(i & ~mask, []).append(i)
    return list(found.values())


def exchange(blocks, axis, bits):
    return lax.all_to_all(
        blocks, axis, 0, 0, tiled=True, axis_index_groups=groups(lax.axis_size(axis), bits)
    )


def crossed(blocks, bits):
    rows, columns = lax.axis_size("row"), lax.axis_size("col")
    found = {}
    for row in range(rows):
        for column in range(columns):
            key = (row & ~sum(bits[column // 2 % 2]), column)
            found.setdefault(key, []).append(row * columns + column)
    return lax.all_to_all(
        blocks, BOTH, 0, 0, tiled=True, axis_index_groups=list(found.values())
    )


def swapped(block):
    return lax.ppermute(block, "col", [(i, i ^ 1) for i in range(lax.axis_size("col"))])


def shifted(block, distance):
    devices = range(lax.axis_size("row"))
    return lax.ppermute(
        block, "row", [(i, i + distance) for i in devices if i + distance in devices]
    )


def neighbours(block):
    rows, columns = lax.axis_size("row"), lax.axis_size("col")
    route = []
    for row in range(rows):
        for column in range(columns):
            to = row + 2 * (column % 2) - 1
            if to in range(rows):
                route.append((row * columns + column, to * columns + column))
    return lax.ppermute(block, BOTH, route)


def repeat_kernel(block, out):
    for i in range(out.shape[0]):
        out[i] = block[...]


def repeated(block, copies):
    return call(repeat_kernel, jax.ShapeDtypeStruct((copies,) + block.shape, block.dtype), block)


def body(
    nodes,
    harmonics,
    grad_blocks,
    pair_rows,
    pair_cols,
    pair_mask,
    block_counts,
    w_left,
    w_right,
    w_harm,
    w_out,
):
    shard, width = nodes.shape
    columns = lax.axis_size("col")
    chips = columns // 2
    share = 24
    spread = 4
    row = lax.axis_index("row")
    core = jnp.bitwise_and(lax.axis_index("col"), 1)
    before, after = shifted(nodes, 1), shifted(nodes, -1)
    row_nodes = exchange(repeated(nodes, columns), "col", COL_BITS).reshape(-1, width)
    places = jnp.stack([block_counts[0, 0], (row - 1) * shard, core]).astype(jnp.int32)
    rows, cols, mask = pair_rows[0], pair_cols[0], pair_mask[0]
    harm, grads = harmonics[0], grad_blocks[0]
    *per_pair, same_nodes = row_pairs(
        places, rows, mask, harm, grads, row_nodes, nodes, w_left, w_harm, w_out
    )
    column_nodes = jnp.concatenate([before, same_nodes, after])
    keep, send, middle, ahead, passed = pair_sums(
        places, rows, cols, mask, harm, grads, row_nodes, column_nodes, w_right, per_pair,
        chips, share,
    )
    parts = (keep + swapped(send)).astype(BF16)
    parts = exchange(parts, "col", CHIP_BITS)
    passed = swapped(passed)
    block, chunks = like(shard, width), like(spread, share, width)
    core = core.reshape(1)
    row_sums, parts, both = call(
        row_kernel, (block, chunks, like(2 * shard, width)), core, parts, ahead, passed, scalars=1
    )
    parts = crossed(parts, (X_BITS, Z_BITS))
    both = neighbours(both)
    parts = call(middle_kernel, chunks, parts)
    parts = crossed(parts, (Z_BITS, X_BITS))
    first = core[0] == 0
    here = jnp.where(first, both[:shard], both[shard:])
    there = swapped(jnp.where(first, both[shard:], both[:shard]))
    shares, column_sums = call(
        last_kernel,
        (jax.ShapeDtypeStruct((chips, share, width), BF16), block),
        parts, middle, here, there,
    )
    grad_nodes = call(node_kernel, block, row_sums, column_sums, w_left, w_right)
    own_shares = exchange(shares, "col", CHIP_BITS)
    left, right, harm, out = split(
        core, own_shares, swapped(own_shares), w_harm.shape[0], w_out.shape[0]
    )
    return (grad_nodes, left, right, harm, out)


def solution(mesh):
    return jax.shard_map(
        body,
        mesh=mesh,
        in_specs=(
            P(BOTH, None),
            P("row", "col", None, None),
            P("row", "col", None, None),
            P("row", "col", None),
            P("row", "col", None),
            P("row", "col", None),
            P("row", "col"),
            P(),
            P(),
            P(),
            P(),
        ),
        out_specs=(P(BOTH, None), P(), P(), P(), P()),
        check_vma=False,
    )
```
